32 devices in a mesh: lat: 16 (over z, y, x), lon: 2 (over core).
Axes of the slice: x: 2, y: 2, z: 4, core: 2. Of those that a mesh axis runs over, the one named last changes fastest.
Arguments:
- ensemble: float32 [81, 10, 32, 256], P(None, None, 'lat', 'lon'), may hold values from -6 to 6
- obs_values: float32 [3, 512], replicated, may hold values from -8 to 8
- obs_errors: float32 [3, 512], replicated, may hold values from 2 to 20
- obs_device: int32 [3, 512], replicated, may hold values from 0 to 31, as said below
- obs_cell: int32 [3, 512], replicated, may hold values from 0 to 2559
- obs_order: int32 [3, 512], replicated, may hold values from 0 to 511, each once within a row
- coupling: int32 [3, 64, 16, 2], P(None, None, 'lat', 'lon'), may hold values 0 or 1
Outputs:
- analysis: float32 [81, 10, 32, 256], P(None, None, 'lat', 'lon')
The draws below stay inside these ranges and needn't reach their ends.
Inputs may be any that keep to these rules, and one draw needn't show every extreme that they name: `obs_device`: in every batch each state group holds at most 32 observations, and some group holds exactly 32.
All inputs are finite; a program needn't handle non-finite values. No bound on the sum of `coupling` on one device may be relied on, other than what follows from the above.
Results may differ from the reference program's by a relative error of at most 0.0003.
Values sent between devices are 32-bit elements; how exact they have to be, the bound alone decides.
A program may use at most 64 MiB of HBM per device.

```python
import math
import jax
import jax.numpy as jnp
from jax import lax

AUG = 81
LEV = 10
LATC = 2
LONC = 128
NBATCH = 3
OBLK = 64
OB = 8
NOBS = 512
NDEV = 32
CAP = 32
N_LAT = 16
N_LON = 2


def draw_obs_device(key, part):
    key = jax.random.fold_in(key, 11)

    def single(batch_key):
        key_first, key_slots, key_shuffle = jax.random.split(batch_key, 3)
        busiest = jax.random.randint(key_first, (), 0, NDEV)
        slots = jax.random.permutation(key_slots, (NDEV - 1) * CAP)[:NOBS - CAP]
        others = slots // CAP
        others = others + (others >= busiest).astype(jnp.int32)
        placed = jnp.concatenate([jnp.full((CAP,), busiest, jnp.int32), others.astype(jnp.int32)])
        return jax.random.permutation(key_shuffle, placed)
    return jax.vmap(single)(jax.random.split(key, NBATCH)).astype(jnp.int32)


def place_ends(array, rng, least, high):
    longest = array.shape.index(max(array.shape))
    spots = []
    for shift in (0, 1):
        where = [jax.random.randint(jax.random.fold_in(rng, axis), (), 0, length) for axis, length in enumerate(array.shape)]
        where[longest] = (where[longest] + shift) % array.shape[longest]
        spots.append(tuple(where))
    return array.at[spots[0]].set(least).at[spots[1]].set(high)


def block_levels(key, shape, cuts, smallest, largest):
    level, own = 1.0, jax.random.fold_in(key, 6)
    for dim, blocks in cuts:
        draws = jnp.exp(jax.random.uniform(jax.random.fold_in(own, dim), (blocks,), jnp.float32, smallest / len(cuts), largest / len(cuts)))
        level = level * jnp.repeat(draws, shape[dim] // blocks).reshape([-1 if axis == dim else 1 for axis in range(len(shape))])
    return level


def noise(own_key, dims, width, reach, shards=(), kind=jnp.bfloat16):
    result = width * jax.random.normal(own_key, dims, jnp.float32)
    if shards:
        result = result * block_levels(own_key, dims, shards, -0.22, 0.18)
    return jnp.clip(result, -reach, reach).astype(kind)


def setup_inputs(seed: int = 0) -> dict:
    arg_keys = jax.random.split(jax.random.key(seed), 8)
    return {
        "ensemble": noise(arg_keys[0], (AUG, LEV, LATC * N_LAT, LONC * N_LON), 1.0, 6.0, ((2, 16), (3, 2)), jnp.float32),
        "obs_values": noise(arg_keys[1], (NBATCH, NOBS), 1.5, 8.0, (), jnp.float32),
        "obs_errors": jnp.clip(jnp.exp(jax.random.uniform(arg_keys[2], (NBATCH, NOBS), jnp.float32, math.log(2.0), math.log(20.0))), 2.0, 20.0),
        "obs_device": draw_obs_device(jax.random.fold_in(arg_keys[7], 71), 0),
        "obs_cell": place_ends(jax.random.randint(arg_keys[4], (NBATCH, NOBS), 0, LEV * LATC * LONC), jax.random.fold_in(arg_keys[4], 1), 0, (LEV * LATC * LONC) - 1).astype(jnp.int32),
        "obs_order": jax.vmap(lambda own: jax.random.permutation(own, NOBS))(jax.random.split(arg_keys[5], NBATCH)).reshape((NBATCH, NOBS)).astype(jnp.int32),
        "coupling": place_ends((jax.random.randint(arg_keys[6], (NBATCH, OBLK, N_LAT, N_LON), 0, 4) < 1).astype(jnp.int32), jax.random.fold_in(arg_keys[6], 1), 0, 1),
    }


HIGH = lax.Precision.HIGHEST

def block_maps(prior_rows, block_ids, values, errors):
    augmented = prior_rows.shape[0]
    members = augmented - 1
    count_blocks = block_ids.shape[0]
    priors_start = jnp.transpose(prior_rows[:, block_ids], (1, 2, 0))
    value_blocks = values[block_ids]
    error_blocks = errors[block_ids]
    identity = jnp.eye(augmented, dtype=jnp.float32)
    identity_stack = jnp.broadcast_to(identity, (count_blocks, augmented, augmented))

    def assimilate(position, product):
        column = lax.dynamic_index_in_dim(priors_start, position, 1, keepdims=False)
        error_now = lax.dynamic_index_in_dim(error_blocks, position, 1, keepdims=False)
        value_now = lax.dynamic_index_in_dim(value_blocks, position, 1, keepdims=False)
        prior = jnp.einsum('bij,bj->bi', product, column, precision=HIGH)
        perturb = prior[:, 1:]
        spread = lax.optimization_barrier(jnp.sum(perturb * perturb, axis=1)) / (members - 1)
        denominator = spread + error_now
        factor_gain = 1.0 / ((members - 1) * denominator)
        shrink = 1.0 / (1.0 + jnp.sqrt(error_now / denominator))
        innovation = value_now - prior[:, 0]
        row_mix = jnp.einsum('bi,bij->bj', perturb, product[:, 1:, :], precision=HIGH)
        column_mix = jnp.concatenate([(factor_gain * innovation)[:, None], -(shrink * factor_gain)[:, None] * perturb], axis=1)
        return product + column_mix[:, :, None] * row_mix[:, None, :]
    return lax.fori_loop(0, block_ids.shape[1], assimilate, identity_stack)

def compose(transforms, coupled_row):
    augmented = transforms.shape[1]
    identity = jnp.eye(augmented, dtype=jnp.float32)
    chosen = jnp.where(coupled_row[:, None, None] > 0, transforms, identity[None])
    while chosen.shape[0] > 1:
        chosen = jnp.einsum('kij,kjl->kil', chosen[1::2], chosen[0::2], precision=HIGH)
    return chosen[0]

def reference(ensemble, obs_values, obs_errors, obs_device, obs_cell, obs_order, coupling):
    augmented, levels, rows_all, cols_all = ensemble.shape
    rows_dev = rows_all // N_LAT
    cols_dev = cols_all // N_LON
    device_blocks = ensemble.reshape(augmented, levels, N_LAT, rows_dev, N_LON, cols_dev)
    device_blocks = device_blocks.transpose(2, 4, 0, 1, 3, 5).reshape(N_LAT * N_LON, augmented, levels * rows_dev * cols_dev)
    coupled = coupling.transpose(0, 2, 3, 1).reshape(NBATCH, N_LAT * N_LON, OBLK)
    for batch in range(NBATCH):
        prior_rows = device_blocks[obs_device[batch], :, obs_cell[batch]].T
        block_ids = obs_order[batch].reshape(OBLK, OB)
        transforms = block_maps(prior_rows, block_ids, obs_values[batch], obs_errors[batch])

        def advance(element):
            members_block, coupled_row = element
            return jnp.dot(compose(transforms, coupled_row), members_block, precision=HIGH)
        device_blocks = lax.map(advance, (device_blocks, coupled[batch]))
    analysis = device_blocks.reshape(N_LAT, N_LON, augmented, levels, rows_dev, cols_dev)
    analysis = analysis.transpose(2, 3, 0, 4, 1, 5).reshape(augmented, levels, rows_all, cols_all)
    return analysis
```

```python
import functools
import jax
import jax.numpy as jnp
from jax import lax
from jax.experimental import pallas as pl
from jax.experimental.pallas import tpu as pltpu
from jax.sharding import PartitionSpec as P

MESH = pl.DeviceIdType.MESH
GROUP = 32
LANES = 128
VMEM_LIMIT = 32 * 1024 * 1024


def digits_of(n_lat, n_lon):
    def factors(size):
        out, stride = [], 1
        while size > 1:
            f = 4 if size % 4 == 0 else (2 if size % 2 == 0 else size)
            out.append((stride, f))
            stride, size = stride * f, size // f
        return out
    if (n_lat, n_lon) == (16, 2):
        return [("lat", 4, 4), ("lat", 1, 2), ("lat", 2, 2), ("lon", 1, 2)]
    return [("lon", s, f) for s, f in factors(n_lon)] + [("lat", s, f) for s, f in factors(n_lat)]


def slab_of(device, digits, n_lon):
    place = {"lat": device // n_lon, "lon": device % n_lon}
    slab, weight = 0, 1
    for axis, stride, size in digits:
        slab = slab + (place[axis] // stride) % size * weight
        weight *= size
    return slab


def split2(a):
    hi = a.astype(jnp.bfloat16)
    return hi, (a - hi.astype(jnp.float32)).astype(jnp.bfloat16)


def mm3(a, b, dims=((1,), (0,))):
    ah, al = a if isinstance(a, tuple) else split2(a)
    bh, bl = b if isinstance(b, tuple) else split2(b)
    dot = functools.partial(
        lax.dot_general, dimension_numbers=(dims, ((), ())), preferred_element_type=jnp.float32
    )
    return dot(ah, bh) + (dot(ah, bl) + dot(al, bh))


NT = ((1,), (1,))


def pick_kernel(nbatch, cap, capp, aug, per_member, rows, cells_ref, state_ref, extra_ref, x_ref):
    lane = lax.broadcasted_iota(jnp.int32, (aug, LANES), 1)

    def one(index, acc):
        cell = cells_ref[index]
        slab = state_ref[pl.ds(cell // LANES, aug, stride=per_member), :]
        moved = pltpu.roll(slab, lax.rem(index - cell % LANES + 2 * LANES, LANES), 1)
        return jnp.where(lane == index, moved, acc)

    picked = lax.fori_loop(0, nbatch * capp, one, jnp.zeros((aug, LANES), jnp.float32))
    padded = jnp.concatenate([picked, jnp.zeros((LANES - aug, LANES), jnp.float32)], axis=0)
    turned = jnp.transpose(padded)
    x_ref[0:rows - nbatch * capp, :] = (
        lax.broadcasted_iota(jnp.int32, (rows - nbatch * capp, LANES), 0)
        == lax.broadcasted_iota(jnp.int32, (rows - nbatch * capp, LANES), 1)
    ).astype(jnp.float32)
    x_ref[rows - nbatch * capp:rows, :] = turned[0:nbatch * capp, :] + extra_ref[...]


def exchange_kernel(digits, cap, offset, x_ref, buf_ref, send_sem, recv_sem):
    place = {axis: lax.axis_index(axis) for axis in ("lat", "lon")}
    mine = [lax.rem(place[axis] // stride, size) for axis, stride, size in digits]

    def peer(which, step):
        axis, stride, size = digits[which]
        other = lax.rem(mine[which] + step, size)
        moved = dict(place)
        moved[axis] = place[axis] + (other - mine[which]) * stride
        return (moved["lat"], moved["lon"])

    barrier = pltpu.get_barrier_semaphore()
    count = 0
    for which, (_, _, size) in enumerate(digits):
        for step in range(1, size):
            pl.semaphore_signal(barrier, inc=1, device_id=peer(which, step), device_id_type=MESH)
            count += 1
    own = tuple(mine[::-1])
    buf_ref[own] = x_ref[offset:offset + cap, :]
    pl.semaphore_wait(barrier, count)

    slots = [0]
    sends = []

    def send(part, device):
        slot = slots[0]
        slots[0] += 1
        copy = pltpu.make_async_remote_copy(
            src_ref=buf_ref.at[part], dst_ref=buf_ref.at[part],
            send_sem=send_sem.at[slot], recv_sem=recv_sem.at[slot],
            device_id=device, device_id_type=MESH,
        )
        copy.start()
        sends.append(copy)
        return copy

    if [size for _, _, size in digits] == [4, 2, 2, 2]:
        z, x, y, k = mine
        first = [send((k, y, x, z), peer(0, step)) for step in (1, 2, 3)]
        for copy in first:
            copy.wait_recv()
        to_x = send((k, y, x), peer(1, 1))
        to_y = send((k, y, x), peer(2, 1))
        last = [send((k, y, x), peer(3, 1))]
        to_x.wait_recv()
        diag = [send((k, y, 1 - x, pl.ds(0, 2)), peer(2, 1))]
        to_y.wait_recv()
        diag.append(send((k, 1 - y, x, pl.ds(2, 2)), peer(1, 1)))
        last.append(send((k, y, 1 - x), peer(3, 1)))
        last.append(send((k, 1 - y, x), peer(3, 1)))
        for copy in diag:
            copy.wait_recv()
        last.append(send((k, 1 - y, 1 - x), peer(3, 1)))
        for copy in last:
            copy.wait_recv()
    else:
        for which, (_, _, size) in enumerate(digits):
            part = tuple(mine[which:][::-1])
            stage = [send(part, peer(which, step)) for step in range(1, size)]
            for copy in stage:
                copy.wait_recv()
    for copy in sends:
        copy.wait_send()


def exchange(x, digits, cap, offset, ident):
    shape = tuple(size for _, _, size in digits[::-1]) + (cap, LANES)
    copies = 16 if [s for _, _, s in digits] == [4, 2, 2, 2] else sum(s - 1 for _, _, s in digits)
    return pl.pallas_call(
        functools.partial(exchange_kernel, digits, cap, offset),
        out_shape=jax.ShapeDtypeStruct(shape, jnp.float32),
        in_specs=[pl.BlockSpec(memory_space=pltpu.VMEM)],
        out_specs=pl.BlockSpec(memory_space=pltpu.VMEM),
        scratch_shapes=[pltpu.SemaphoreType.DMA((copies,)), pltpu.SemaphoreType.DMA((copies,))],
        compiler_params=pltpu.CompilerParams(
            collective_id=ident, has_side_effects=True, vmem_limit_bytes=VMEM_LIMIT
        ),
        name="exchange",
    )(x)


def group_update(z, valid, x, per_block, members):
    lane = lax.broadcasted_iota(jnp.int32, (GROUP, LANES), 1)
    is_member = (lane >= 1) & (lane <= members)
    z = list(z)
    hs, vs, ws = [], [], []
    for i in range(per_block):
        p = z[i]
        h = jnp.where(is_member, p, 0.0)
        s = jnp.sum(h * h, axis=1, keepdims=True) / (members - 1)
        y = p[:, members + 1:members + 2]
        r = p[:, members + 2:members + 3]
        q = s + r
        c = 1.0 / ((members - 1) * q)
        a = 1.0 / (1.0 + jnp.sqrt(r / q))
        d = y - p[:, 0:1]
        v = jnp.where(lane == 0, c * d, -(a * c) * h)
        for j in range(i + 1, per_block):
            z[j] = z[j] + v * jnp.sum(h * z[j], axis=1, keepdims=True)
        w = h
        for j in range(i):
            w = w + ws[j] * jnp.sum(h * vs[j], axis=1, keepdims=True)
        vs.append(v)
        ws.append(w)
    v_all = split2(jnp.concatenate([v * valid for v in vs], axis=0))
    w_all = split2(jnp.concatenate(ws, axis=0))
    size = per_block * GROUP
    upper = mm3(v_all, w_all, NT)
    row = lax.broadcasted_iota(jnp.int32, (size, size), 0) & (GROUP - 1)
    col = lax.broadcasted_iota(jnp.int32, (size, size), 1) & (GROUP - 1)
    differ = row ^ col
    levels = GROUP.bit_length() - 1
    ahead = row < col
    inverse = jnp.where(
        lax.broadcasted_iota(jnp.int32, (size, size), 0)
        == lax.broadcasted_iota(jnp.int32, (size, size), 1), 1.0,
        jnp.where(ahead & (differ == 1), upper, 0.0),
    )
    for level in range(1, levels):
        pairs = ahead & (differ >= (1 << level)) & (differ < (2 << level))
        parts = split2(inverse)
        inverse = inverse + mm3(mm3(parts, jnp.where(pairs, upper, 0.0)), parts)
    return x + mm3(mm3(mm3(x, w_all, NT), inverse), v_all)


def update_kernel(batch, per_block, members, count_ref, list_ref, pos_ref, x_ref, buf_ref, out_ref, z_ref):
    out_ref[...] = x_ref[...]
    total = count_ref[batch]

    @pl.loop(0, (total + GROUP - 1) // GROUP)
    def _(group):
        start = group * GROUP

        @pl.loop(0, GROUP)
        def _(b):
            block = list_ref[batch, start + b]
            for i in range(per_block):
                source = pos_ref[batch, block * per_block + i]
                z_ref[pl.ds(i * GROUP + b, 1), :] = buf_ref[pl.ds(source, 1), :]

        valid = (
            start + lax.broadcasted_iota(jnp.int32, (GROUP, 1), 0) < total
        ).astype(jnp.float32)
        z = [z_ref[i * GROUP:(i + 1) * GROUP, :] for i in range(per_block)]
        out_ref[...] = group_update(z, valid, out_ref[...], per_block, members)


def final_kernel(aug, per_member, x_ref, state_ref, out_ref):
    turned = jnp.transpose(x_ref[0:LANES, :])
    parts = split2(turned[0:aug, 0:aug])
    for j in range(0, per_member, 2):
        cut = [state_ref[pl.ds(j + k, aug, stride=per_member), :] for k in range(2)]
        new = mm3(parts, jnp.concatenate(cut, axis=1))
        for k in range(2):
            out_ref[pl.ds(j + k, aug, stride=per_member), :] = new[:, k * LANES:(k + 1) * LANES]


def vspec():
    return pl.BlockSpec(memory_space=pltpu.VMEM)


def sspec():
    return pl.BlockSpec(memory_space=pltpu.SMEM)


def local(ensemble, obs_values, obs_errors, obs_device, obs_cell, obs_order, coupling):
    aug, levels, rows_dev, cols_dev = ensemble.shape
    members = aug - 1
    n_lat, n_lon = lax.axis_size("lat"), lax.axis_size("lon")
    ndev = n_lat * n_lon
    nbatch, nobs = obs_values.shape
    nblocks = coupling.shape[1]
    per_block = nobs // nblocks
    cap = max(1, 2 * nobs // ndev)
    capp = -(-cap // 8) * 8
    digits = digits_of(n_lat, n_lon)
    me = lax.axis_index("lat") * n_lon + lax.axis_index("lon")
    per_member = levels * rows_dev * cols_dev // LANES
    state = ensemble.reshape(aug * per_member, LANES)
    params = pltpu.CompilerParams(vmem_limit_bytes=VMEM_LIMIT)

    same = obs_device[:, :, None] == obs_device[:, None, :]
    before = lax.iota(jnp.int32, nobs)[None, :] < lax.iota(jnp.int32, nobs)[:, None]
    rank = jnp.sum((same & before[None]).astype(jnp.int32), axis=2)
    pos = slab_of(obs_device, digits, n_lon) * cap + rank
    pos_sorted = jnp.take_along_axis(pos, obs_order, axis=1)
    slots = lax.iota(jnp.int32, capp)
    chosen = (obs_device == me)[:, None, :] & (rank[:, None, :] == slots[None, :, None])
    cells = jnp.sum(jnp.where(chosen, obs_cell[:, None, :], 0), axis=2).reshape(nbatch * capp)
    value_own = jnp.sum(jnp.where(chosen, obs_values[:, None, :], 0.0), axis=2).reshape(nbatch * capp, 1)
    error_own = jnp.sum(jnp.where(chosen, obs_errors[:, None, :], 0.0), axis=2).reshape(nbatch * capp, 1)
    lanes = lax.iota(jnp.int32, LANES)[None, :]
    extra = jnp.where(lanes == aug, value_own, jnp.where(lanes == aug + 1, error_own, 0.0))

    coupled = coupling.reshape(nbatch, nblocks) > 0
    blocks = lax.iota(jnp.int32, nblocks)
    earlier = jnp.sum((coupled[:, None, :] & (blocks[None, :] < blocks[:, None])[None]).astype(jnp.int32), axis=2)
    count = jnp.sum(coupled.astype(jnp.int32), axis=1)
    hit = coupled[:, None, :] & (earlier[:, None, :] == blocks[None, :, None])
    listed = jnp.sum(jnp.where(hit, blocks[None, None, :], 0), axis=2)
    if nblocks % GROUP:
        listed = jnp.pad(listed, ((0, 0), (0, GROUP - nblocks % GROUP)))

    base = LANES
    rows = base + nbatch * capp
    x = pl.pallas_call(
        functools.partial(pick_kernel, nbatch, cap, capp, aug, per_member, rows),
        out_shape=jax.ShapeDtypeStruct((rows, LANES), jnp.float32),
        in_specs=[sspec(), vspec(), vspec()],
        out_specs=vspec(),
        compiler_params=params,
        name="pick",
    )(cells, state, extra)

    for batch in range(nbatch):
        buf = exchange(x, digits, cap, base + batch * capp, batch)
        x = pl.pallas_call(
            functools.partial(update_kernel, batch, per_block, members),
            out_shape=jax.ShapeDtypeStruct((rows, LANES), jnp.float32),
            in_specs=[sspec(), sspec(), sspec(), vspec(), vspec()],
            out_specs=vspec(),
            scratch_shapes=[pltpu.VMEM((per_block * GROUP, LANES), jnp.float32)],
            compiler_params=params,
            name="update",
        )(count, listed, pos_sorted, x, buf.reshape(ndev * cap, LANES))

    out = pl.pallas_call(
        functools.partial(final_kernel, aug, per_member),
        out_shape=jax.ShapeDtypeStruct((aug * per_member, LANES), jnp.float32),
        in_specs=[vspec(), vspec()],
        out_specs=vspec(),
        compiler_params=params,
        name="final",
    )(x, state)
    return out.reshape(aug, levels, rows_dev, cols_dev)


def solution(mesh):
    placed = (P(None, None, "lat", "lon"), P(), P(), P(), P(), P(), P(None, None, "lat", "lon"))
    return jax.shard_map(
        local, mesh=mesh, in_specs=placed, out_specs=P(None, None, "lat", "lon"), check_vma=False
    )
```

```python
import functools
import jax
import jax.numpy as jnp
from jax import lax
from jax.experimental import pallas as pl
from jax.experimental.pallas import tpu as pltpu
from jax.sharding import PartitionSpec as P

MESH = pl.DeviceIdType.MESH
GROUP = 32
LANES = 128
VMEM_LIMIT = 32 * 1024 * 1024


def digits_of(n_lat, n_lon):
    def factors(size):
        out, stride = [], 1
        while size > 1:
            f = 4 if size % 4 == 0 else (2 if size % 2 == 0 else size)
            out.append((stride, f))
            stride, size = stride * f, size // f
        return out
    if (n_lat, n_lon) == (16, 2):
        return [("lat", 4, 4), ("lat", 1, 2), ("lat", 2, 2), ("lon", 1, 2)]
    return [("lon", s, f) for s, f in factors(n_lon)] + [("lat", s, f) for s, f in factors(n_lat)]


def split2(a):
    hi = a.astype(jnp.bfloat16)
    return hi, (a - hi.astype(jnp.float32)).astype(jnp.bfloat16)


def mm3(a, b, dims=((1,), (0,))):
    ah, al = a if isinstance(a, tuple) else split2(a)
    bh, bl = b if isinstance(b, tuple) else split2(b)
    dot = functools.partial(
        lax.dot_general, dimension_numbers=(dims, ((), ())), preferred_element_type=jnp.float32
    )
    return dot(ah, bh) + (dot(ah, bl) + dot(al, bh))


NT = ((1,), (1,))


def pow2_part(value, stride, size):
    return (value >> (stride.bit_length() - 1)) & (size - 1)


def exchange_body(digits, fill, meanwhile, buf_ref, send_sem, recv_sem):
    place = {axis: lax.axis_index(axis) for axis in ("lat", "lon")}
    mine = [lax.rem(place[axis] // stride, size) for axis, stride, size in digits]

    def peer(*moves):
        moved = dict(place)
        for which, step in moves:
            axis, stride, size = digits[which]
            other = lax.rem(mine[which] + step, size)
            moved[axis] = moved[axis] + (other - mine[which]) * stride
        return (moved["lat"], moved["lon"])

    grid = [size for _, _, size in digits] == [4, 2, 2, 2]
    partners = [((which, step),) for which, (_, _, size) in enumerate(digits) for step in range(1, size)]
    if grid:
        partners.append(((1, 1), (2, 1)))
    barrier = pltpu.get_barrier_semaphore()
    for moves in partners:
        pl.semaphore_signal(barrier, inc=1, device_id=peer(*moves), device_id_type=MESH)
    own = tuple(mine[::-1])
    buf_ref[own] = fill()
    pl.semaphore_wait(barrier, len(partners))

    sends = []

    def send(part, device):
        slot = len(sends)
        copy = pltpu.make_async_remote_copy(
            src_ref=buf_ref.at[part], dst_ref=buf_ref.at[part],
            send_sem=send_sem.at[slot], recv_sem=recv_sem.at[slot],
            device_id=device, device_id_type=MESH,
        )
        copy.start()
        sends.append(copy)
        return copy

    if grid:
        z, x, y, k = mine
        plane = [peer((1, 1)), peer((2, 1)), peer((1, 1), (2, 1))]
        other = peer((3, 1))
        line = [(step, send((k, y, x, z), peer((0, step)))) for step in (1, 3, 2)]
        arriving = [[send((k, y, x, z), device)] for device in plane]
        meanwhile()
        for step, copy in line:
            copy.wait_recv()
            chunk = lax.rem(z + 4 - step, 4)
            for place_now, device in enumerate(plane):
                arriving[place_now].append(send((k, y, x, chunk), device))
        last = [send((k, y, x), other)]
        for copies, (yy, xx) in zip(arriving, ((y, 1 - x), (1 - y, x), (1 - y, 1 - x))):
            for copy in copies:
                copy.wait_recv()
            last.append(send((k, yy, xx), other))
        for copy in last:
            copy.wait_recv()
    else:
        for which, (_, _, size) in enumerate(digits):
            part = tuple(mine[which:][::-1])
            stage = [send(part, peer((which, step))) for step in range(1, size)]
            if which == 0:
                meanwhile()
            for copy in stage:
                copy.wait_recv()
    for copy in sends:
        copy.wait_send()


def exchange_kernel(digits, cap, offset, x_ref, buf_ref, send_sem, recv_sem):
    exchange_body(
        digits, lambda: x_ref[offset:offset + cap, :], lambda: None, buf_ref, send_sem, recv_sem
    )


def exchange_scratch(digits):
    copies = 19 if [s for _, _, s in digits] == [4, 2, 2, 2] else sum(s - 1 for _, _, s in digits)
    return [pltpu.SemaphoreType.DMA((copies,)), pltpu.SemaphoreType.DMA((copies,))]


def buffer_shape(digits, cap):
    return jax.ShapeDtypeStruct(
        tuple(size for _, _, size in digits[::-1]) + (cap, LANES), jnp.float32
    )


def exchange(x, digits, cap, offset, ident):
    return pl.pallas_call(
        functools.partial(exchange_kernel, digits, cap, offset),
        out_shape=buffer_shape(digits, cap),
        in_specs=[vspec()],
        out_specs=vspec(),
        scratch_shapes=exchange_scratch(digits),
        compiler_params=pltpu.CompilerParams(
            collective_id=ident, has_side_effects=True, vmem_limit_bytes=VMEM_LIMIT
        ),
        name="exchange",
    )(x)


def first_kernel(digits, cap, capp, aug, per_member, base, values_ref, errors_ref, device_ref, cell_ref,
                 state_ref, buf_ref, x_ref, pos_ref, send_sem, recv_sem):
    nbatch, nobs = device_ref.shape
    n_lat, n_lon = lax.axis_size("lat"), lax.axis_size("lon")
    ndev = n_lat * n_lon
    me = lax.axis_index("lat") * n_lon + lax.axis_index("lon")
    earlier = (
        lax.broadcasted_iota(jnp.int32, (nobs, nobs), 0) < lax.broadcasted_iota(jnp.int32, (nobs, nobs), 1)
    ).astype(jnp.float32).astype(jnp.bfloat16)

    def ranks(flags):
        return jnp.dot(flags.astype(jnp.bfloat16), earlier, preferred_element_type=jnp.float32)

    def fill():
        owned = (device_ref[...] == me).astype(jnp.float32)
        rank = ranks(owned)
        slot = lax.broadcasted_iota(jnp.int32, (capp, nobs), 0).astype(jnp.float32)
        lane = lax.broadcasted_iota(jnp.int32, (capp, LANES), 1)
        cells = []
        for batch in range(nbatch):
            row = slice(batch, batch + 1)
            chosen = (rank[row] == slot) & (owned[row] > 0)

            def total(ref):
                return jnp.sum(jnp.where(chosen, ref[row, :].astype(jnp.float32), 0.0), axis=1, keepdims=True)

            cells.append(total(cell_ref))
            x_ref[base + batch * capp:base + (batch + 1) * capp, :] = jnp.where(
                lane == aug, total(values_ref), jnp.where(lane == aug + 1, total(errors_ref), 0.0)
            )
        cell = jnp.concatenate(cells, axis=0).astype(jnp.int32)
        wide = 2 * LANES
        spot = lax.broadcasted_iota(jnp.int32, (nbatch * capp, wide), 1)
        picked = jnp.zeros((nbatch * capp, aug), jnp.float32)
        for j in range(0, per_member, 2):
            cut = jnp.concatenate(
                [state_ref[pl.ds(j + k, aug, stride=per_member), :] for k in range(2)], axis=1
            )
            mark = (spot + j * LANES == cell).astype(jnp.float32).astype(jnp.bfloat16)
            for _ in range(3):
                part = cut.astype(jnp.bfloat16)
                picked = picked + lax.dot_general(
                    mark, part, (NT, ((), ())), preferred_element_type=jnp.float32
                )
                cut = cut - part.astype(jnp.float32)
        x_ref[base:base + nbatch * capp, 0:aug] = picked
        return x_ref[base:base + cap, :]

    def meanwhile():
        x_ref[0:base, :] = (
            lax.broadcasted_iota(jnp.int32, (base, LANES), 0)
            == lax.broadcasted_iota(jnp.int32, (base, LANES), 1)
        ).astype(jnp.float32)
        names = lax.broadcasted_iota(jnp.int32, (ndev, nobs), 0)
        for batch in range(nbatch):
            device = device_ref[batch:batch + 1, :]
            held = (device == names).astype(jnp.float32)
            rank = jnp.sum(held * ranks(held), axis=0, keepdims=True)
            place = {"lat": device >> (n_lon.bit_length() - 1), "lon": device & (n_lon - 1)}
            slab, weight = jnp.zeros_like(device), 1
            for axis, stride, size in digits:
                slab = slab + pow2_part(place[axis], stride, size) * weight
                weight *= size
            pos_ref[batch:batch + 1, :] = slab * cap + rank.astype(jnp.int32)

    exchange_body(digits, fill, meanwhile, buf_ref, send_sem, recv_sem)


def group_update(z, valid, x, per_block, members):
    lane = lax.broadcasted_iota(jnp.int32, (GROUP, LANES), 1)
    is_member = (lane >= 1) & (lane <= members)
    z = list(z)
    hs, vs, ws = [], [], []
    for i in range(per_block):
        p = z[i]
        h = jnp.where(is_member, p, 0.0)
        s = jnp.sum(h * h, axis=1, keepdims=True) / (members - 1)
        y = p[:, members + 1:members + 2]
        r = p[:, members + 2:members + 3]
        q = s + r
        c = 1.0 / ((members - 1) * q)
        a = 1.0 / (1.0 + jnp.sqrt(r / q))
        d = y - p[:, 0:1]
        v = jnp.where(lane == 0, c * d, -(a * c) * h)
        for j in range(i + 1, per_block):
            z[j] = z[j] + v * jnp.sum(h * z[j], axis=1, keepdims=True)
        w = h
        for j in range(i):
            w = w + ws[j] * jnp.sum(h * vs[j], axis=1, keepdims=True)
        vs.append(v)
        ws.append(w)
    v_all = split2(jnp.concatenate([v * valid for v in vs], axis=0))
    w_all = split2(jnp.concatenate(ws, axis=0))
    size = per_block * GROUP
    upper = mm3(v_all, w_all, NT)
    row = lax.broadcasted_iota(jnp.int32, (size, size), 0) & (GROUP - 1)
    col = lax.broadcasted_iota(jnp.int32, (size, size), 1) & (GROUP - 1)
    differ = row ^ col
    levels = GROUP.bit_length() - 1
    ahead = row < col
    inverse = jnp.where(
        lax.broadcasted_iota(jnp.int32, (size, size), 0)
        == lax.broadcasted_iota(jnp.int32, (size, size), 1), 1.0,
        jnp.where(ahead & (differ == 1), upper, 0.0),
    )
    for level in range(1, levels):
        pairs = ahead & (differ >= (1 << level)) & (differ < (2 << level))
        parts = split2(inverse)
        inverse = inverse + mm3(mm3(parts, jnp.where(pairs, upper, 0.0)), parts)
    return x + mm3(mm3(mm3(x, w_all, NT), inverse), v_all)


def update_kernel(batch, per_block, members, coupled_ref, order_ref, pos_ref, x_ref, buf_ref, out_ref, z_ref, list_ref):
    out_ref[...] = x_ref[...]
    total = jnp.int32(0)
    for block in range(coupled_ref.shape[1]):
        list_ref[total] = block
        total = total + (coupled_ref[batch, block] > 0).astype(jnp.int32)

    @pl.loop(0, (total + GROUP - 1) // GROUP)
    def _(group):
        start = group * GROUP

        @pl.loop(0, GROUP, unroll=8)
        def _(b):
            block = list_ref[jnp.minimum(start + b, total - 1)]
            for i in range(per_block):
                source = pos_ref[batch, order_ref[batch, block * per_block + i]]
                z_ref[pl.ds(i * GROUP + b, 1), :] = buf_ref[pl.ds(source, 1), :]

        valid = (
            start + lax.broadcasted_iota(jnp.int32, (GROUP, 1), 0) < total
        ).astype(jnp.float32)
        z = [z_ref[i * GROUP:(i + 1) * GROUP, :] for i in range(per_block)]
        out_ref[...] = group_update(z, valid, out_ref[...], per_block, members)


def final_kernel(aug, per_member, x_ref, state_ref, out_ref):
    turned = jnp.transpose(x_ref[0:LANES, :])
    parts = split2(turned[0:aug, 0:aug])
    for j in range(0, per_member, 2):
        cut = [state_ref[pl.ds(j + k, aug, stride=per_member), :] for k in range(2)]
        new = mm3(parts, jnp.concatenate(cut, axis=1))
        for k in range(2):
            out_ref[pl.ds(j + k, aug, stride=per_member), :] = new[:, k * LANES:(k + 1) * LANES]


def vspec():
    return pl.BlockSpec(memory_space=pltpu.VMEM)


def sspec():
    return pl.BlockSpec(memory_space=pltpu.SMEM)


def local(ensemble, obs_values, obs_errors, obs_device, obs_cell, obs_order, coupling):
    aug, levels, rows_dev, cols_dev = ensemble.shape
    members = aug - 1
    n_lat, n_lon = lax.axis_size("lat"), lax.axis_size("lon")
    ndev = n_lat * n_lon
    nbatch, nobs = obs_values.shape
    nblocks = coupling.shape[1]
    per_block = nobs // nblocks
    cap = max(1, 2 * nobs // ndev)
    capp = -(-cap // 8) * 8
    digits = digits_of(n_lat, n_lon)
    per_member = levels * rows_dev * cols_dev // LANES
    state = ensemble.reshape(aug * per_member, LANES)
    params = pltpu.CompilerParams(vmem_limit_bytes=VMEM_LIMIT)

    coupled = coupling.reshape(nbatch, nblocks)
    base = LANES
    rows = base + nbatch * capp
    buf, x, pos = pl.pallas_call(
        functools.partial(first_kernel, digits, cap, capp, aug, per_member, base),
        out_shape=(
            buffer_shape(digits, cap),
            jax.ShapeDtypeStruct((rows, LANES), jnp.float32),
            jax.ShapeDtypeStruct((nbatch, nobs), jnp.int32),
        ),
        in_specs=[vspec()] * 5,
        out_specs=(vspec(),) * 3,
        scratch_shapes=exchange_scratch(digits),
        compiler_params=pltpu.CompilerParams(
            collective_id=0, has_side_effects=True, vmem_limit_bytes=VMEM_LIMIT
        ),
        name="first",
    )(obs_values, obs_errors, obs_device, obs_cell, state)

    for batch in range(nbatch):
        if batch > 0:
            buf = exchange(x, digits, cap, base + batch * capp, batch)
        x = pl.pallas_call(
            functools.partial(update_kernel, batch, per_block, members),
            out_shape=jax.ShapeDtypeStruct((rows, LANES), jnp.float32),
            in_specs=[sspec(), sspec(), sspec(), vspec(), vspec()],
            out_specs=vspec(),
            scratch_shapes=[
                pltpu.VMEM((per_block * GROUP, LANES), jnp.float32),
                pltpu.SMEM((nblocks + 1,), jnp.int32),
            ],
            compiler_params=params,
            name="update",
        )(coupled, obs_order, pos, x, buf.reshape(ndev * cap, LANES))

    out = pl.pallas_call(
        functools.partial(final_kernel, aug, per_member),
        out_shape=jax.ShapeDtypeStruct((aug * per_member, LANES), jnp.float32),
        in_specs=[vspec(), vspec()],
        out_specs=vspec(),
        compiler_params=params,
        name="final",
    )(x, state)
    return out.reshape(aug, levels, rows_dev, cols_dev)


def solution(mesh):
    placed = (P(None, None, "lat", "lon"), P(), P(), P(), P(), P(), P(None, None, "lat", "lon"))
    return jax.shard_map(
        local, mesh=mesh, in_specs=placed, out_specs=P(None, None, "lat", "lon"), check_vma=False
    )
```

```python
import functools
import itertools
import jax
import jax.numpy as jnp
from jax import lax
from jax.experimental import pallas as pl
from jax.experimental.pallas import tpu as pltpu
from jax.sharding import PartitionSpec as P

MESH = pl.DeviceIdType.MESH
GROUP = 32
LANES = 128
VMEM_LIMIT = 32 * 1024 * 1024


def digits_of(n_lat, n_lon):
    def factors(size):
        out, stride = [], 1
        while size > 1:
            f = 4 if size % 4 == 0 else (2 if size % 2 == 0 else size)
            out.append((stride, f))
            stride, size = stride * f, size // f
        return out
    if (n_lat, n_lon) == (16, 2):
        return [("lat", 4, 4), ("lat", 1, 2), ("lat", 2, 2), ("lon", 1, 2)]
    return [("lon", s, f) for s, f in factors(n_lon)] + [("lat", s, f) for s, f in factors(n_lat)]


def split2(a):
    hi = a.astype(jnp.bfloat16)
    return hi, (a - hi.astype(jnp.float32)).astype(jnp.bfloat16)


def mm3(a, b, dims=((1,), (0,))):
    ah, al = a if isinstance(a, tuple) else split2(a)
    bh, bl = b if isinstance(b, tuple) else split2(b)
    dot = functools.partial(
        lax.dot_general, dimension_numbers=(dims, ((), ())), preferred_element_type=jnp.float32
    )
    return dot(ah, bh) + (dot(ah, bl) + dot(al, bh))


NT = ((1,), (1,))


def pow2_part(value, stride, size):
    return (value >> (stride.bit_length() - 1)) & (size - 1)


def fold_of(cap, width):
    return 24 if cap == 32 and LANES - width >= (width + 1) // 2 else cap


def exchange_body(digits, cap, width, fill, meanwhile, buf_ref, send_sem, recv_sem):
    place = {axis: lax.axis_index(axis) for axis in ("lat", "lon")}
    mine = [lax.rem(place[axis] // stride, size) for axis, stride, size in digits]

    def peer(*moves):
        moved = dict(place)
        for which, step in moves:
            axis, stride, size = digits[which]
            other = lax.rem(mine[which] + step, size)
            moved[axis] = moved[axis] + (other - mine[which]) * stride
        return (moved["lat"], moved["lon"])

    grid = [size for _, _, size in digits] == [4, 2, 2, 2]
    partners = [((which, step),) for which, (_, _, size) in enumerate(digits) for step in range(1, size)]
    if grid:
        partners.append(((1, 1), (2, 1)))
    barrier = pltpu.get_barrier_semaphore()
    for moves in partners:
        pl.semaphore_signal(barrier, inc=1, device_id=peer(*moves), device_id_type=MESH)
    own = tuple(mine[::-1])
    sent = fold_of(cap, width)
    half = (width + 1) // 2
    chunk_now = fill()
    if sent < cap:
        tail = chunk_now[24:32]
        lane = lax.broadcasted_iota(jnp.int32, tail.shape, 1)
        low = jnp.where(lane < half, tail, 0.0)
        high = jnp.where((lane >= half) & (lane < width), tail, 0.0)
        buf_ref[own + (slice(0, 8),)] = chunk_now[0:8] + pltpu.roll(low, width, 1)
        buf_ref[own + (slice(8, 16),)] = chunk_now[8:16] + pltpu.roll(high, width - half, 1)
        buf_ref[own + (slice(16, 24),)] = chunk_now[16:24]
    else:
        buf_ref[own] = chunk_now
    pl.semaphore_wait(barrier, len(partners))

    sends = []

    def send(part, device):
        slot = len(sends)
        part = part + (slice(None),) * (len(digits) - len(part)) + (pl.ds(0, sent),)
        copy = pltpu.make_async_remote_copy(
            src_ref=buf_ref.at[part], dst_ref=buf_ref.at[part],
            send_sem=send_sem.at[slot], recv_sem=recv_sem.at[slot],
            device_id=device, device_id_type=MESH,
        )
        copy.start()
        sends.append(copy)
        return copy

    if grid:
        z, x, y, k = mine
        plane = [peer((1, 1)), peer((2, 1)), peer((1, 1), (2, 1))]
        other = peer((3, 1))
        line = [(step, send((k, y, x, z), peer((0, step)))) for step in (1, 3, 2)]
        arriving = [[send((k, y, x, z), device)] for device in plane]
        meanwhile()
        for step, copy in line:
            copy.wait_recv()
            chunk = lax.rem(z + 4 - step, 4)
            for place_now, device in enumerate(plane):
                arriving[place_now].append(send((k, y, x, chunk), device))
        last = [send((k, y, x), other)]
        for copies, (yy, xx) in zip(arriving, ((y, 1 - x), (1 - y, x), (1 - y, 1 - x))):
            for copy in copies:
                copy.wait_recv()
            last.append(send((k, yy, xx), other))
        for copy in last:
            copy.wait_recv()
    else:
        for which, (_, _, size) in enumerate(digits):
            part = tuple(mine[which:][::-1])
            stage = [send(part, peer((which, step))) for step in range(1, size)]
            if which == 0:
                meanwhile()
            for copy in stage:
                copy.wait_recv()
    for copy in sends:
        copy.wait_send()
    if sent < cap:
        for spot in itertools.product(*(range(size) for _, _, size in digits[::-1])):
            low = pltpu.roll(buf_ref[spot + (slice(0, 8),)], LANES - width, 1)
            high = pltpu.roll(buf_ref[spot + (slice(8, 16),)], LANES - width + half, 1)
            lane = lax.broadcasted_iota(jnp.int32, low.shape, 1)
            buf_ref[spot + (slice(24, 32),)] = jnp.where(lane < half, low, high)


def exchange_kernel(digits, cap, width, x_ref, buf_ref, send_sem, recv_sem):
    exchange_body(
        digits, cap, width, lambda: x_ref[0:cap, :], lambda: None, buf_ref, send_sem, recv_sem
    )


def exchange_scratch(digits):
    copies = 19 if [s for _, _, s in digits] == [4, 2, 2, 2] else sum(s - 1 for _, _, s in digits)
    return [pltpu.SemaphoreType.DMA((copies,)), pltpu.SemaphoreType.DMA((copies,))]


def buffer_shape(digits, cap):
    return jax.ShapeDtypeStruct(
        tuple(size for _, _, size in digits[::-1]) + (cap, LANES), jnp.float32
    )


def exchange(x, digits, cap, width, ident):
    return pl.pallas_call(
        functools.partial(exchange_kernel, digits, cap, width),
        out_shape=buffer_shape(digits, cap),
        in_specs=[vspec()],
        out_specs=vspec(),
        scratch_shapes=exchange_scratch(digits),
        compiler_params=pltpu.CompilerParams(
            collective_id=ident, has_side_effects=True, vmem_limit_bytes=VMEM_LIMIT
        ),
        name="exchange",
    )(x)


def first_kernel(digits, cap, capp, aug, per_member, base, values_ref, errors_ref, device_ref, cell_ref,
                 state_ref, buf_ref, x_ref, pos_ref, send_sem, recv_sem):
    nbatch, nobs = device_ref.shape
    n_lat, n_lon = lax.axis_size("lat"), lax.axis_size("lon")
    ndev = n_lat * n_lon
    me = lax.axis_index("lat") * n_lon + lax.axis_index("lon")
    earlier = (
        lax.broadcasted_iota(jnp.int32, (nobs, nobs), 0) < lax.broadcasted_iota(jnp.int32, (nobs, nobs), 1)
    ).astype(jnp.float32).astype(jnp.bfloat16)

    def ranks(flags):
        return jnp.dot(flags.astype(jnp.bfloat16), earlier, preferred_element_type=jnp.float32)

    def fill():
        owned = (device_ref[...] == me).astype(jnp.float32)
        rank = ranks(owned)
        slot = lax.broadcasted_iota(jnp.int32, (capp, nobs), 0).astype(jnp.float32)
        lane = lax.broadcasted_iota(jnp.int32, (capp, LANES), 1)
        cells = []
        for batch in range(nbatch):
            row = slice(batch, batch + 1)
            chosen = (rank[row] == slot) & (owned[row] > 0)

            def total(ref):
                return jnp.sum(jnp.where(chosen, ref[row, :].astype(jnp.float32), 0.0), axis=1, keepdims=True)

            cells.append(total(cell_ref))
            x_ref[batch * capp:(batch + 1) * capp, :] = jnp.where(
                lane == aug, total(values_ref), jnp.where(lane == aug + 1, total(errors_ref), 0.0)
            )
        cell = jnp.concatenate(cells, axis=0).astype(jnp.int32)
        wide = 2 * LANES
        spot = lax.broadcasted_iota(jnp.int32, (nbatch * capp, wide), 1)
        picked = jnp.zeros((nbatch * capp, aug), jnp.float32)
        for j in range(0, per_member, 2):
            cut = jnp.concatenate(
                [state_ref[pl.ds(j + k, aug, stride=per_member), :] for k in range(2)], axis=1
            )
            mark = (spot + j * LANES == cell).astype(jnp.float32).astype(jnp.bfloat16)
            for _ in range(3):
                part = cut.astype(jnp.bfloat16)
                picked = picked + lax.dot_general(
                    mark, part, (NT, ((), ())), preferred_element_type=jnp.float32
                )
                cut = cut - part.astype(jnp.float32)
        x_ref[0:base, 0:aug] = picked
        return x_ref[0:cap, :]

    def meanwhile():
        square = (x_ref.shape[0] - base, LANES)
        x_ref[base:, :] = (
            lax.broadcasted_iota(jnp.int32, square, 0) == lax.broadcasted_iota(jnp.int32, square, 1)
        ).astype(jnp.float32)
        names = lax.broadcasted_iota(jnp.int32, (ndev, nobs), 0)
        for batch in range(nbatch):
            device = device_ref[batch:batch + 1, :]
            held = (device == names).astype(jnp.float32)
            rank = jnp.sum(held * ranks(held), axis=0, keepdims=True)
            place = {"lat": device >> (n_lon.bit_length() - 1), "lon": device & (n_lon - 1)}
            slab, weight = jnp.zeros_like(device), 1
            for axis, stride, size in digits:
                slab = slab + pow2_part(place[axis], stride, size) * weight
                weight *= size
            pos_ref[batch:batch + 1, :] = slab * cap + rank.astype(jnp.int32)

    exchange_body(digits, cap, aug + 2, fill, meanwhile, buf_ref, send_sem, recv_sem)


def group_update(z, valid, x, per_block, members):
    lane = lax.broadcasted_iota(jnp.int32, (GROUP, LANES), 1)
    is_member = (lane >= 1) & (lane <= members)
    z = list(z)
    hs, vs, ws = [], [], []
    for i in range(per_block):
        p = z[i]
        h = jnp.where(is_member, p, 0.0)
        s = jnp.sum(h * h, axis=1, keepdims=True) / (members - 1)
        y = p[:, members + 1:members + 2]
        r = p[:, members + 2:members + 3]
        q = s + r
        c = 1.0 / ((members - 1) * q)
        a = 1.0 / (1.0 + jnp.sqrt(r / q))
        d = y - p[:, 0:1]
        v = jnp.where(lane == 0, c * d, -(a * c) * h)
        for j in range(i + 1, per_block):
            z[j] = z[j] + v * jnp.sum(h * z[j], axis=1, keepdims=True)
        w = h
        for j in range(i):
            w = w + ws[j] * jnp.sum(h * vs[j], axis=1, keepdims=True)
        vs.append(v)
        ws.append(w)
    half = GROUP // 2
    size = per_block * half
    row_id = lax.broadcasted_iota(jnp.int32, (size, size), 0)
    col_id = lax.broadcasted_iota(jnp.int32, (size, size), 1)
    differ = (row_id ^ col_id) & (half - 1)
    ahead = (row_id & (half - 1)) < (col_id & (half - 1))
    levels = half.bit_length() - 1
    vs = [v * valid for v in vs]
    cuts = [slice(0, half), slice(half, GROUP)]
    v_half = [split2(jnp.concatenate([v[cut] for v in vs], axis=0)) for cut in cuts]
    w_half = [split2(jnp.concatenate([w[cut] for w in ws], axis=0)) for cut in cuts]
    upper = [mm3(v, w, NT) for v, w in zip(v_half, w_half)]
    across = split2(mm3(v_half[0], w_half[1], NT))
    x_parts = split2(x)
    seen = [mm3(x_parts, w, NT) for w in w_half]
    inverse = [
        jnp.where(row_id == col_id, 1.0, jnp.where(ahead & (differ == 1), u, 0.0)) for u in upper
    ]
    for level in range(1, levels):
        pairs = ahead & (differ >= (1 << level)) & (differ < (2 << level))
        parts = [split2(i) for i in inverse]
        inner = [mm3(p, jnp.where(pairs, u, 0.0)) for p, u in zip(parts, upper)]
        inverse = [i + mm3(m, p) for i, m, p in zip(inverse, inner, parts)]
    first = split2(mm3(seen[0], inverse[0]))
    second = mm3(seen[1] + mm3(first, across), inverse[1])
    return x + (mm3(first, v_half[0]) + mm3(second, v_half[1]))


def update_kernel(batch, per_block, members, capp, coupled_ref, order_ref, pos_ref, x_ref, buf_ref, out_ref, z_ref, list_ref):
    out_ref[...] = x_ref[capp:, :]
    total = jnp.int32(0)
    for block in range(coupled_ref.shape[1]):
        list_ref[total] = block
        total = total + (coupled_ref[batch, block] > 0).astype(jnp.int32)

    @pl.loop(0, (total + GROUP - 1) // GROUP)
    def _(group):
        start = group * GROUP

        @pl.loop(0, GROUP, unroll=8)
        def _(b):
            block = list_ref[jnp.minimum(start + b, total - 1)]
            for i in range(per_block):
                source = pos_ref[batch, order_ref[batch, block * per_block + i]]
                z_ref[pl.ds(i * GROUP + b, 1), :] = buf_ref[pl.ds(source, 1), :]

        valid = (
            start + lax.broadcasted_iota(jnp.int32, (GROUP, 1), 0) < total
        ).astype(jnp.float32)
        z = [z_ref[i * GROUP:(i + 1) * GROUP, :] for i in range(per_block)]
        out_ref[...] = group_update(z, valid, out_ref[...], per_block, members)


def final_kernel(aug, per_member, x_ref, state_ref, out_ref):
    rest = jnp.zeros((LANES - x_ref.shape[0], LANES), jnp.float32)
    turned = jnp.transpose(jnp.concatenate([x_ref[...], rest], axis=0))
    parts = split2(turned[0:aug, 0:aug])
    for j in range(0, per_member, 2):
        cut = [state_ref[pl.ds(j + k, aug, stride=per_member), :] for k in range(2)]
        new = mm3(parts, jnp.concatenate(cut, axis=1))
        for k in range(2):
            out_ref[pl.ds(j + k, aug, stride=per_member), :] = new[:, k * LANES:(k + 1) * LANES]


def vspec():
    return pl.BlockSpec(memory_space=pltpu.VMEM)


def sspec():
    return pl.BlockSpec(memory_space=pltpu.SMEM)


def local(ensemble, obs_values, obs_errors, obs_device, obs_cell, obs_order, coupling):
    aug, levels, rows_dev, cols_dev = ensemble.shape
    members = aug - 1
    n_lat, n_lon = lax.axis_size("lat"), lax.axis_size("lon")
    ndev = n_lat * n_lon
    nbatch, nobs = obs_values.shape
    nblocks = coupling.shape[1]
    per_block = nobs // nblocks
    cap = max(1, 2 * nobs // ndev)
    capp = -(-cap // 8) * 8
    digits = digits_of(n_lat, n_lon)
    per_member = levels * rows_dev * cols_dev // LANES
    state = ensemble.reshape(aug * per_member, LANES)
    params = pltpu.CompilerParams(vmem_limit_bytes=VMEM_LIMIT)

    coupled = coupling.reshape(nbatch, nblocks)
    base = nbatch * capp
    rows = base + -(-aug // 16) * 16
    buf, x, pos = pl.pallas_call(
        functools.partial(first_kernel, digits, cap, capp, aug, per_member, base),
        out_shape=(
            buffer_shape(digits, cap),
            jax.ShapeDtypeStruct((rows, LANES), jnp.float32),
            jax.ShapeDtypeStruct((nbatch, nobs), jnp.int32),
        ),
        in_specs=[vspec()] * 5,
        out_specs=(vspec(),) * 3,
        scratch_shapes=exchange_scratch(digits),
        compiler_params=pltpu.CompilerParams(
            collective_id=0, has_side_effects=True, vmem_limit_bytes=VMEM_LIMIT
        ),
        name="first",
    )(obs_values, obs_errors, obs_device, obs_cell, state)

    for batch in range(nbatch):
        if batch > 0:
            buf = exchange(x, digits, cap, aug + 2, batch)
        x = pl.pallas_call(
            functools.partial(update_kernel, batch, per_block, members, capp),
            out_shape=jax.ShapeDtypeStruct((rows - (batch + 1) * capp, LANES), jnp.float32),
            in_specs=[sspec(), sspec(), sspec(), vspec(), vspec()],
            out_specs=vspec(),
            scratch_shapes=[
                pltpu.VMEM((per_block * GROUP, LANES), jnp.float32),
                pltpu.SMEM((nblocks + 1,), jnp.int32),
            ],
            compiler_params=params,
            name="update",
        )(coupled, obs_order, pos, x, buf.reshape(ndev * cap, LANES))

    out = pl.pallas_call(
        functools.partial(final_kernel, aug, per_member),
        out_shape=jax.ShapeDtypeStruct((aug * per_member, LANES), jnp.float32),
        in_specs=[vspec(), vspec()],
        out_specs=vspec(),
        compiler_params=params,
        name="final",
    )(x, state)
    return out.reshape(aug, levels, rows_dev, cols_dev)


def solution(mesh):
    placed = (P(None, None, "lat", "lon"), P(), P(), P(), P(), P(), P(None, None, "lat", "lon"))
    return jax.shard_map(
        local, mesh=mesh, in_specs=placed, out_specs=P(None, None, "lat", "lon"), check_vma=False
    )
```

```python
import functools
import itertools
import jax
import jax.numpy as jnp
from jax import lax
from jax.experimental import pallas as pl
from jax.experimental.pallas import tpu as pltpu
from jax.sharding import PartitionSpec as P

MESH = pl.DeviceIdType.MESH
GROUP = 32
LANES = 128
PLANE = ((0, 0), (1, 0), (0, 1), (1, 1))
VMEM_LIMIT = 32 * 1024 * 1024


def digits_of(n_lat, n_lon):
    def factors(size):
        out, stride = [], 1
        while size > 1:
            f = 4 if size % 4 == 0 else (2 if size % 2 == 0 else size)
            out.append((stride, f))
            stride, size = stride * f, size // f
        return out
    if (n_lat, n_lon) == (16, 2):
        return [("lat", 4, 4), ("lat", 1, 2), ("lat", 2, 2), ("lon", 1, 2)]
    return [("lon", s, f) for s, f in factors(n_lon)] + [("lat", s, f) for s, f in factors(n_lat)]


def split2(a):
    hi = a.astype(jnp.bfloat16)
    return hi, (a - hi.astype(jnp.float32)).astype(jnp.bfloat16)


def mm3(a, b, dims=((1,), (0,))):
    ah, al = a if isinstance(a, tuple) else split2(a)
    bh, bl = b if isinstance(b, tuple) else split2(b)
    dot = functools.partial(
        lax.dot_general, dimension_numbers=(dims, ((), ())), preferred_element_type=jnp.float32
    )
    return dot(ah, bh) + (dot(ah, bl) + dot(al, bh))


NT = ((1,), (1,))


def pow2_part(value, stride, size):
    return (value >> (stride.bit_length() - 1)) & (size - 1)


def fold_of(cap, width):
    return 24 if cap == 32 and LANES - width >= (width + 1) // 2 else cap


def exchange_body(digits, cap, width, fill, meanwhile, buf_ref, send_sem, recv_sem):
    place = {axis: lax.axis_index(axis) for axis in ("lat", "lon")}
    mine = [lax.rem(place[axis] // stride, size) for axis, stride, size in digits]

    def peer(*moves):
        moved = dict(place)
        for which, step in moves:
            axis, stride, size = digits[which]
            other = lax.rem(mine[which] + step, size)
            moved[axis] = moved[axis] + (other - mine[which]) * stride
        return (moved["lat"], moved["lon"])

    grid = [size for _, _, size in digits] == [4, 2, 2, 2]
    partners = [((which, step),) for which, (_, _, size) in enumerate(digits) for step in range(1, size)]
    spread = [(dz, turn) for dz in (2, 1, 3, 0) for turn in PLANE[::-1] if dz or any(turn)]
    if grid:
        partners = [((0, dz), (1, dx), (2, dy)) for dz, (dx, dy) in spread] + [((3, 1),)]
    barrier = pltpu.get_barrier_semaphore()
    for moves in partners:
        pl.semaphore_signal(barrier, inc=1, device_id=peer(*moves), device_id_type=MESH)
    own = tuple(mine[::-1])
    sent = fold_of(cap, width)
    half = (width + 1) // 2
    chunk_now = fill()
    if sent < cap:
        tail = chunk_now[24:32]
        lane = lax.broadcasted_iota(jnp.int32, tail.shape, 1)
        low = jnp.where(lane < half, tail, 0.0)
        high = jnp.where((lane >= half) & (lane < width), tail, 0.0)
        buf_ref[own + (slice(0, 8),)] = chunk_now[0:8] + pltpu.roll(low, width, 1)
        buf_ref[own + (slice(8, 16),)] = chunk_now[8:16] + pltpu.roll(high, width - half, 1)
        buf_ref[own + (slice(16, 24),)] = chunk_now[16:24]
    else:
        buf_ref[own] = chunk_now
    pl.semaphore_wait(barrier, len(partners))

    sends = []

    def send(part, device):
        slot = len(sends)
        part = part + (slice(None),) * (len(digits) - len(part)) + (pl.ds(0, sent),)
        copy = pltpu.make_async_remote_copy(
            src_ref=buf_ref.at[part], dst_ref=buf_ref.at[part],
            send_sem=send_sem.at[slot], recv_sem=recv_sem.at[slot],
            device_id=device, device_id_type=MESH,
        )
        copy.start()
        sends.append(copy)
        return copy

    if grid:
        z, x, y, k = mine
        other = peer((3, 1))
        arriving = {turn: [] for turn in PLANE}
        for dz, (dx, dy) in spread:
            arriving[dx, dy].append(send((k, y, x, z), peer((0, dz), (1, dx), (2, dy))))
        meanwhile()
        last = []
        for dx, dy in PLANE:
            for copy in arriving[dx, dy]:
                copy.wait_recv()
            last.append(send((k, lax.rem(y + dy, 2), lax.rem(x + dx, 2)), other))
        for copy in last:
            copy.wait_recv()
    else:
        for which, (_, _, size) in enumerate(digits):
            part = tuple(mine[which:][::-1])
            stage = [send(part, peer((which, step))) for step in range(1, size)]
            if which == 0:
                meanwhile()
            for copy in stage:
                copy.wait_recv()
    for copy in sends:
        copy.wait_send()
    if sent < cap:
        for spot in itertools.product(*(range(size) for _, _, size in digits[::-1])):
            low = pltpu.roll(buf_ref[spot + (slice(0, 8),)], LANES - width, 1)
            high = pltpu.roll(buf_ref[spot + (slice(8, 16),)], LANES - width + half, 1)
            lane = lax.broadcasted_iota(jnp.int32, low.shape, 1)
            buf_ref[spot + (slice(24, 32),)] = jnp.where(lane < half, low, high)


def exchange_kernel(digits, cap, width, x_ref, buf_ref, send_sem, recv_sem):
    exchange_body(
        digits, cap, width, lambda: x_ref[0:cap, :], lambda: None, buf_ref, send_sem, recv_sem
    )


def exchange_scratch(digits):
    copies = 19 if [s for _, _, s in digits] == [4, 2, 2, 2] else sum(s - 1 for _, _, s in digits)
    return [pltpu.SemaphoreType.DMA((copies,)), pltpu.SemaphoreType.DMA((copies,))]


def buffer_shape(digits, cap):
    return jax.ShapeDtypeStruct(
        tuple(size for _, _, size in digits[::-1]) + (cap, LANES), jnp.float32
    )


def exchange(x, digits, cap, width, ident):
    return pl.pallas_call(
        functools.partial(exchange_kernel, digits, cap, width),
        out_shape=buffer_shape(digits, cap),
        in_specs=[vspec()],
        out_specs=vspec(),
        scratch_shapes=exchange_scratch(digits),
        compiler_params=pltpu.CompilerParams(
            collective_id=ident, has_side_effects=True, vmem_limit_bytes=VMEM_LIMIT
        ),
        name="exchange",
    )(x)


def first_kernel(digits, cap, capp, aug, per_member, base, values_ref, errors_ref, device_ref, cell_ref,
                 state_ref, buf_ref, x_ref, pos_ref, send_sem, recv_sem):
    nbatch, nobs = device_ref.shape
    n_lat, n_lon = lax.axis_size("lat"), lax.axis_size("lon")
    ndev = n_lat * n_lon
    me = lax.axis_index("lat") * n_lon + lax.axis_index("lon")
    earlier = (
        lax.broadcasted_iota(jnp.int32, (nobs, nobs), 0) < lax.broadcasted_iota(jnp.int32, (nobs, nobs), 1)
    ).astype(jnp.float32).astype(jnp.bfloat16)

    def ranks(flags):
        return jnp.dot(flags.astype(jnp.bfloat16), earlier, preferred_element_type=jnp.float32)

    def fill():
        owned = (device_ref[...] == me).astype(jnp.float32)
        rank = ranks(owned)
        slot = lax.broadcasted_iota(jnp.int32, (capp, nobs), 0).astype(jnp.float32)
        lane = lax.broadcasted_iota(jnp.int32, (capp, LANES), 1)
        cells = []
        for batch in range(nbatch):
            row = slice(batch, batch + 1)
            chosen = (rank[row] == slot) & (owned[row] > 0)

            def total(ref):
                return jnp.sum(jnp.where(chosen, ref[row, :].astype(jnp.float32), 0.0), axis=1, keepdims=True)

            cells.append(total(cell_ref))
            x_ref[batch * capp:(batch + 1) * capp, :] = jnp.where(
                lane == aug, total(values_ref), jnp.where(lane == aug + 1, total(errors_ref), 0.0)
            )
        cell = jnp.concatenate(cells, axis=0).astype(jnp.int32)
        wide = 2 * LANES
        spot = lax.broadcasted_iota(jnp.int32, (nbatch * capp, wide), 1)
        picked = jnp.zeros((nbatch * capp, aug), jnp.float32)
        for j in range(0, per_member, 2):
            cut = jnp.concatenate(
                [state_ref[pl.ds(j + k, aug, stride=per_member), :] for k in range(2)], axis=1
            )
            mark = (spot + j * LANES == cell).astype(jnp.float32).astype(jnp.bfloat16)
            for _ in range(3):
                part = cut.astype(jnp.bfloat16)
                picked = picked + lax.dot_general(
                    mark, part, (NT, ((), ())), preferred_element_type=jnp.float32
                )
                cut = cut - part.astype(jnp.float32)
        x_ref[0:base, 0:aug] = picked
        return x_ref[0:cap, :]

    def meanwhile():
        square = (x_ref.shape[0] - base, LANES)
        x_ref[base:, :] = (
            lax.broadcasted_iota(jnp.int32, square, 0) == lax.broadcasted_iota(jnp.int32, square, 1)
        ).astype(jnp.float32)
        names = lax.broadcasted_iota(jnp.int32, (ndev, nobs), 0)
        for batch in range(nbatch):
            device = device_ref[batch:batch + 1, :]
            held = (device == names).astype(jnp.float32)
            rank = jnp.sum(held * ranks(held), axis=0, keepdims=True)
            place = {"lat": device >> (n_lon.bit_length() - 1), "lon": device & (n_lon - 1)}
            slab, weight = jnp.zeros_like(device), 1
            for axis, stride, size in digits:
                slab = slab + pow2_part(place[axis], stride, size) * weight
                weight *= size
            pos_ref[batch:batch + 1, :] = slab * cap + rank.astype(jnp.int32)

    exchange_body(digits, cap, aug + 2, fill, meanwhile, buf_ref, send_sem, recv_sem)


def group_update(z, valid, x, per_block, members):
    lane = lax.broadcasted_iota(jnp.int32, (GROUP, LANES), 1)
    is_member = (lane >= 1) & (lane <= members)
    z = list(z)
    hs, vs, ws = [], [], []
    for i in range(per_block):
        p = z[i]
        h = jnp.where(is_member, p, 0.0)
        s = jnp.sum(h * h, axis=1, keepdims=True) / (members - 1)
        y = p[:, members + 1:members + 2]
        r = p[:, members + 2:members + 3]
        q = s + r
        c = 1.0 / ((members - 1) * q)
        a = 1.0 / (1.0 + jnp.sqrt(r / q))
        d = y - p[:, 0:1]
        v = jnp.where(lane == 0, c * d, -(a * c) * h)
        for j in range(i + 1, per_block):
            z[j] = z[j] + v * jnp.sum(h * z[j], axis=1, keepdims=True)
        w = h
        for j in range(i):
            w = w + ws[j] * jnp.sum(h * vs[j], axis=1, keepdims=True)
        vs.append(v)
        ws.append(w)
    half = GROUP // 2
    size = per_block * half
    row_id = lax.broadcasted_iota(jnp.int32, (size, size), 0)
    col_id = lax.broadcasted_iota(jnp.int32, (size, size), 1)
    differ = (row_id ^ col_id) & (half - 1)
    ahead = (row_id & (half - 1)) < (col_id & (half - 1))
    levels = half.bit_length() - 1
    vs = [v * valid for v in vs]
    cuts = [slice(0, half), slice(half, GROUP)]
    v_half = [split2(jnp.concatenate([v[cut] for v in vs], axis=0)) for cut in cuts]
    w_half = [split2(jnp.concatenate([w[cut] for w in ws], axis=0)) for cut in cuts]
    upper = [mm3(v, w, NT) for v, w in zip(v_half, w_half)]
    across = split2(mm3(v_half[0], w_half[1], NT))
    x_parts = split2(x)
    seen = [mm3(x_parts, w, NT) for w in w_half]
    inverse = [
        jnp.where(row_id == col_id, 1.0, jnp.where(ahead & (differ == 1), u, 0.0)) for u in upper
    ]
    for level in range(1, levels):
        pairs = ahead & (differ >= (1 << level)) & (differ < (2 << level))
        parts = [split2(i) for i in inverse]
        inner = [mm3(p, jnp.where(pairs, u, 0.0)) for p, u in zip(parts, upper)]
        inverse = [i + mm3(m, p) for i, m, p in zip(inverse, inner, parts)]
    first = split2(mm3(seen[0], inverse[0]))
    second = mm3(seen[1] + mm3(first, across), inverse[1])
    return x + (mm3(first, v_half[0]) + mm3(second, v_half[1]))


def update_kernel(batch, per_block, members, capp, coupled_ref, order_ref, pos_ref, x_ref, buf_ref, out_ref, z_ref, list_ref):
    out_ref[...] = x_ref[capp:, :]
    total = jnp.int32(0)
    for block in range(coupled_ref.shape[1]):
        list_ref[total] = block
        total = total + (coupled_ref[batch, block] > 0).astype(jnp.int32)

    @pl.loop(0, (total + GROUP - 1) // GROUP)
    def _(group):
        start = group * GROUP

        @pl.loop(0, GROUP, unroll=8)
        def _(b):
            block = list_ref[jnp.minimum(start + b, total - 1)]
            for i in range(per_block):
                source = pos_ref[batch, order_ref[batch, block * per_block + i]]
                z_ref[pl.ds(i * GROUP + b, 1), :] = buf_ref[pl.ds(source, 1), :]

        valid = (
            start + lax.broadcasted_iota(jnp.int32, (GROUP, 1), 0) < total
        ).astype(jnp.float32)
        z = [z_ref[i * GROUP:(i + 1) * GROUP, :] for i in range(per_block)]
        out_ref[...] = group_update(z, valid, out_ref[...], per_block, members)


def final_kernel(aug, per_member, x_ref, state_ref, out_ref):
    rest = jnp.zeros((LANES - x_ref.shape[0], LANES), jnp.float32)
    turned = jnp.transpose(jnp.concatenate([x_ref[...], rest], axis=0))
    parts = split2(turned[0:aug, 0:aug])
    for j in range(0, per_member, 2):
        cut = [state_ref[pl.ds(j + k, aug, stride=per_member), :] for k in range(2)]
        new = mm3(parts, jnp.concatenate(cut, axis=1))
        for k in range(2):
            out_ref[pl.ds(j + k, aug, stride=per_member), :] = new[:, k * LANES:(k + 1) * LANES]


def vspec():
    return pl.BlockSpec(memory_space=pltpu.VMEM)


def sspec():
    return pl.BlockSpec(memory_space=pltpu.SMEM)


def local(ensemble, obs_values, obs_errors, obs_device, obs_cell, obs_order, coupling):
    aug, levels, rows_dev, cols_dev = ensemble.shape
    members = aug - 1
    n_lat, n_lon = lax.axis_size("lat"), lax.axis_size("lon")
    ndev = n_lat * n_lon
    nbatch, nobs = obs_values.shape
    nblocks = coupling.shape[1]
    per_block = nobs // nblocks
    cap = max(1, 2 * nobs // ndev)
    capp = -(-cap // 8) * 8
    digits = digits_of(n_lat, n_lon)
    per_member = levels * rows_dev * cols_dev // LANES
    state = ensemble.reshape(aug * per_member, LANES)
    params = pltpu.CompilerParams(vmem_limit_bytes=VMEM_LIMIT)

    coupled = coupling.reshape(nbatch, nblocks)
    base = nbatch * capp
    rows = base + -(-aug // 16) * 16
    buf, x, pos = pl.pallas_call(
        functools.partial(first_kernel, digits, cap, capp, aug, per_member, base),
        out_shape=(
            buffer_shape(digits, cap),
            jax.ShapeDtypeStruct((rows, LANES), jnp.float32),
            jax.ShapeDtypeStruct((nbatch, nobs), jnp.int32),
        ),
        in_specs=[vspec()] * 5,
        out_specs=(vspec(),) * 3,
        scratch_shapes=exchange_scratch(digits),
        compiler_params=pltpu.CompilerParams(
            collective_id=0, has_side_effects=True, vmem_limit_bytes=VMEM_LIMIT
        ),
        name="first",
    )(obs_values, obs_errors, obs_device, obs_cell, state)

    for batch in range(nbatch):
        if batch > 0:
            buf = exchange(x, digits, cap, aug + 2, batch)
        x = pl.pallas_call(
            functools.partial(update_kernel, batch, per_block, members, capp),
            out_shape=jax.ShapeDtypeStruct((rows - (batch + 1) * capp, LANES), jnp.float32),
            in_specs=[sspec(), sspec(), sspec(), vspec(), vspec()],
            out_specs=vspec(),
            scratch_shapes=[
                pltpu.VMEM((per_block * GROUP, LANES), jnp.float32),
                pltpu.SMEM((nblocks + 1,), jnp.int32),
            ],
            compiler_params=params,
            name="update",
        )(coupled, obs_order, pos, x, buf.reshape(ndev * cap, LANES))

    out = pl.pallas_call(
        functools.partial(final_kernel, aug, per_member),
        out_shape=jax.ShapeDtypeStruct((aug * per_member, LANES), jnp.float32),
        in_specs=[vspec(), vspec()],
        out_specs=vspec(),
        compiler_params=params,
        name="final",
    )(x, state)
    return out.reshape(aug, levels, rows_dev, cols_dev)


def solution(mesh):
    placed = (P(None, None, "lat", "lon"), P(), P(), P(), P(), P(), P(None, None, "lat", "lon"))
    return jax.shard_map(
        local, mesh=mesh, in_specs=placed, out_specs=P(None, None, "lat", "lon"), check_vma=False
    )
```

```python
import functools
import jax
import jax.numpy as jnp
from jax import lax
from jax.experimental import pallas as pl
from jax.experimental.pallas import tpu as pltpu
from jax.sharding import PartitionSpec as P

MESH = pl.DeviceIdType.MESH
GROUP = 32
LANES = 128
PLANE = ((0, 0), (1, 0), (0, 1), (1, 1))
VMEM_LIMIT = 32 * 1024 * 1024


def digits_of(n_lat, n_lon):
    def factors(size):
        out, stride = [], 1
        while size > 1:
            f = 4 if size % 4 == 0 else (2 if size % 2 == 0 else size)
            out.append((stride, f))
            stride, size = stride * f, size // f
        return out
    if (n_lat, n_lon) == (16, 2):
        return [("lat", 4, 4), ("lat", 1, 2), ("lat", 2, 2), ("lon", 1, 2)]
    return [("lon", s, f) for s, f in factors(n_lon)] + [("lat", s, f) for s, f in factors(n_lat)]


def split2(a):
    hi = a.astype(jnp.bfloat16)
    return hi, (a - hi.astype(jnp.float32)).astype(jnp.bfloat16)


def mm3(a, b, dims=((1,), (0,))):
    ah, al = a if isinstance(a, tuple) else split2(a)
    bh, bl = b if isinstance(b, tuple) else split2(b)
    dot = functools.partial(
        lax.dot_general, dimension_numbers=(dims, ((), ())), preferred_element_type=jnp.float32
    )
    return dot(ah, bh) + (dot(ah, bl) + dot(al, bh))


NT = ((1,), (1,))


def pow2_part(value, stride, size):
    return (value >> (stride.bit_length() - 1)) & (size - 1)


def fold_of(cap, width):
    return 24 if cap == 32 and LANES - width >= (width + 1) // 2 else cap


def is_grid(digits):
    return [size for _, _, size in digits] == [4, 2, 2, 2]


class Exchange:
    def __init__(self, digits, cap, width):
        self.digits, self.cap, self.width = digits, cap, width
        self.sent = fold_of(cap, width)
        self.place = {axis: lax.axis_index(axis) for axis in ("lat", "lon")}
        self.mine = [lax.rem(self.place[axis] // stride, size) for axis, stride, size in digits]
        self.weights = [1]
        for _, _, size in digits:
            self.weights.append(self.weights[-1] * size)
        if is_grid(digits):
            self.spread = [(dz, turn) for dz in (2, 1, 3, 0) for turn in PLANE[::-1] if dz or any(turn)]
            self.partners = [((0, dz), (1, dx), (2, dy)) for dz, (dx, dy) in self.spread] + [((3, 1),)]
        else:
            self.partners = [
                ((which, step),) for which, (_, _, size) in enumerate(digits) for step in range(1, size)
            ]

    def peer(self, *moves):
        moved = dict(self.place)
        for which, step in moves:
            axis, stride, size = self.digits[which]
            other = lax.rem(self.mine[which] + step, size)
            moved[axis] = moved[axis] + (other - self.mine[which]) * stride
        return (moved["lat"], moved["lon"])

    def greet(self):
        barrier = pltpu.get_barrier_semaphore()
        for moves in self.partners:
            pl.semaphore_signal(barrier, inc=1, device_id=self.peer(*moves), device_id_type=MESH)

    def await_greetings(self):
        pl.semaphore_wait(pltpu.get_barrier_semaphore(), len(self.partners))

    def place_own(self, chunk, buf_ref):
        width, sent = self.width, self.sent
        half = (width + 1) // 2
        own = sum(digit * weight for digit, weight in zip(self.mine, self.weights))
        if sent < self.cap:
            tail = chunk[24:32]
            lane = lax.broadcasted_iota(jnp.int32, tail.shape, 1)
            low = jnp.where(lane < half, tail, 0.0)
            high = jnp.where((lane >= half) & (lane < width), tail, 0.0)
            buf_ref[own, 0:8] = chunk[0:8] + pltpu.roll(low, width, 1)
            buf_ref[own, 8:16] = chunk[8:16] + pltpu.roll(high, width - half, 1)
            buf_ref[own, 16:24] = chunk[16:24]
        else:
            buf_ref[own] = chunk

    def run(self, buf_ref, send_sem, recv_sem, meanwhile=lambda: None):
        digits, mine, weights, sent = self.digits, self.mine, self.weights, self.sent
        sends = []

        def send(start, count, device):
            slot = len(sends)
            part = buf_ref.at[pl.ds(start, count), pl.ds(0, sent)]
            copy = pltpu.make_async_remote_copy(
                src_ref=part, dst_ref=part, send_sem=send_sem.at[slot], recv_sem=recv_sem.at[slot],
                device_id=device, device_id_type=MESH,
            )
            copy.start()
            sends.append(copy)
            return copy

        if is_grid(digits):
            z, x, y, k = mine
            arriving = {turn: [] for turn in PLANE}
            for dz, (dx, dy) in self.spread:
                own = z + 4 * x + 8 * y + 16 * k
                arriving[dx, dy].append(send(own, 1, self.peer((0, dz), (1, dx), (2, dy))))
            meanwhile()
            last = []
            for dx, dy in PLANE:
                for copy in arriving[dx, dy]:
                    copy.wait_recv()
                start = 4 * lax.rem(x + dx, 2) + 8 * lax.rem(y + dy, 2) + 16 * k
                last.append(send(start, 4, self.peer((3, 1))))
            for copy in last:
                copy.wait_recv()
        else:
            for which, (_, _, size) in enumerate(digits):
                start = sum(mine[i] * weights[i] for i in range(which, len(digits)))
                stage = [send(start, weights[which], self.peer((which, step))) for step in range(1, size)]
                if which == 0:
                    meanwhile()
                for copy in stage:
                    copy.wait_recv()
        for copy in sends:
            copy.wait_send()
        if sent < self.cap:
            width = self.width
            half = (width + 1) // 2
            for spot in range(weights[-1]):
                low = pltpu.roll(buf_ref[spot, 0:8], LANES - width, 1)
                high = pltpu.roll(buf_ref[spot, 8:16], LANES - width + half, 1)
                lane = lax.broadcasted_iota(jnp.int32, low.shape, 1)
                buf_ref[spot, 24:32] = jnp.where(lane < half, low, high)


def exchange_kernel(digits, cap, width, x_ref, buf_ref, send_sem, recv_sem):
    trade = Exchange(digits, cap, width)
    trade.greet()
    trade.place_own(x_ref[0:cap, :], buf_ref)
    trade.await_greetings()
    trade.run(buf_ref, send_sem, recv_sem)


def exchange_scratch(digits):
    copies = 19 if is_grid(digits) else sum(s - 1 for _, _, s in digits)
    return [pltpu.SemaphoreType.DMA((copies,)), pltpu.SemaphoreType.DMA((copies,))]


def exchange(x, digits, cap, width, ident, ndev):
    return pl.pallas_call(
        functools.partial(exchange_kernel, digits, cap, width),
        out_shape=jax.ShapeDtypeStruct((ndev, cap, LANES), jnp.float32),
        in_specs=[vspec()],
        out_specs=vspec(),
        scratch_shapes=exchange_scratch(digits),
        compiler_params=pltpu.CompilerParams(
            collective_id=ident, has_side_effects=True, vmem_limit_bytes=VMEM_LIMIT
        ),
        name="exchange",
    )(x)


def first_kernel(digits, cap, capp, aug, per_member, base, per_block, values_ref, errors_ref,
                 device_ref, cell_ref, order_ref, coupled_ref, state_ref, buf_ref, x_ref, source_ref, count_ref,
                 send_sem, recv_sem):
    trade = Exchange(digits, cap, aug + 3)
    trade.greet()
    nbatch, nobs = device_ref.shape
    n_lat, n_lon = lax.axis_size("lat"), lax.axis_size("lon")
    ndev = n_lat * n_lon
    me = lax.axis_index("lat") * n_lon + lax.axis_index("lon")
    earlier = (
        lax.broadcasted_iota(jnp.int32, (nobs, nobs), 0) < lax.broadcasted_iota(jnp.int32, (nobs, nobs), 1)
    ).astype(jnp.float32).astype(jnp.bfloat16)

    def ranks(flags):
        return jnp.dot(flags.astype(jnp.bfloat16), earlier, preferred_element_type=jnp.float32)

    def fill():
        owned = (device_ref[...] == me).astype(jnp.float32)
        rank = ranks(owned)
        slot = lax.broadcasted_iota(jnp.int32, (capp, nobs), 0).astype(jnp.float32)
        lane = lax.broadcasted_iota(jnp.int32, (capp, LANES), 1)
        cells = []
        most = jnp.max(jnp.sum(coupled_ref[...].astype(jnp.float32), axis=1, keepdims=True), axis=0, keepdims=True)
        for batch in range(nbatch):
            row = slice(batch, batch + 1)
            chosen = (rank[row] == slot) & (owned[row] > 0)

            def total(ref):
                return jnp.sum(jnp.where(chosen, ref[row, :].astype(jnp.float32), 0.0), axis=1, keepdims=True)

            cells.append(total(cell_ref))
            x_ref[batch * capp:(batch + 1) * capp, :] = jnp.where(
                lane == aug, total(values_ref), jnp.where(
                    lane == aug + 1, total(errors_ref), jnp.where(lane == aug + 2, most, 0.0)
                )
            )
        cell = jnp.concatenate(cells, axis=0).astype(jnp.int32)
        wide = 2 * LANES
        spot = lax.broadcasted_iota(jnp.int32, (nbatch * capp, wide), 1)
        picked = jnp.zeros((nbatch * capp, aug), jnp.float32)
        for j in range(0, per_member, 2):
            cut = jnp.concatenate(
                [state_ref[pl.ds(j + k, aug, stride=per_member), :] for k in range(2)], axis=1
            )
            mark = (spot + j * LANES == cell).astype(jnp.float32).astype(jnp.bfloat16)
            for _ in range(3):
                part = cut.astype(jnp.bfloat16)
                picked = picked + lax.dot_general(
                    mark, part, (NT, ((), ())), preferred_element_type=jnp.float32
                )
                cut = cut - part.astype(jnp.float32)
        x_ref[0:base, 0:aug] = picked
        return x_ref[0:cap, :]

    def meanwhile():
        square = (x_ref.shape[0] - base, LANES)
        x_ref[base:, :] = (
            lax.broadcasted_iota(jnp.int32, square, 0) == lax.broadcasted_iota(jnp.int32, square, 1)
        ).astype(jnp.float32)
        names = lax.broadcasted_iota(jnp.int32, (ndev, nobs), 0)
        names_obs = lax.broadcasted_iota(jnp.int32, (nobs, nobs), 0)
        targets = ranks(coupled_ref[...].astype(jnp.float32))
        for batch in range(nbatch):
            device = device_ref[batch:batch + 1, :]
            held = (device == names).astype(jnp.float32)
            rank = jnp.sum(held * ranks(held), axis=0, keepdims=True)
            place = {"lat": device >> (n_lon.bit_length() - 1), "lon": device & (n_lon - 1)}
            slab, weight = jnp.zeros_like(device), 1
            for axis, stride, size in digits:
                slab = slab + pow2_part(place[axis], stride, size) * weight
                weight *= size
            pos = slab * cap + rank.astype(jnp.int32)
            part = lax.broadcasted_iota(jnp.int32, (8, nobs), 0)
            parts = jnp.where(part == 0, pos & 63, jnp.where(part == 1, (pos >> 6) & 63, pos >> 12))
            parts = jnp.where(part < 3, parts, 0).astype(jnp.float32).astype(jnp.bfloat16)
            named = (order_ref[batch:batch + 1, :] == names_obs).astype(jnp.float32).astype(jnp.bfloat16)
            ordered = jnp.dot(parts, named, preferred_element_type=jnp.float32)
            goes = (targets[batch:batch + 1, :] == names_obs.astype(jnp.float32)) & (
                coupled_ref[batch:batch + 1, :] > 0
            )
            packed = lax.dot_general(
                ordered.astype(jnp.bfloat16), goes.astype(jnp.float32).astype(jnp.bfloat16), (NT, ((), ())),
                preferred_element_type=jnp.float32,
            ).astype(jnp.int32)
            source_ref[batch:batch + 1, :] = packed[0:1] + 64 * packed[1:2] + 4096 * packed[2:3]
            count_ref[batch] = jnp.sum(coupled_ref[batch:batch + 1, :]) // per_block

    trade.place_own(fill(), buf_ref)
    trade.await_greetings()
    trade.run(buf_ref, send_sem, recv_sem, meanwhile)
    most = buf_ref[0, 0:1]
    for spot in range(1, ndev):
        most = jnp.maximum(most, buf_ref[spot, 0:1])
    lane = lax.broadcasted_iota(jnp.int32, (1, LANES), 1)
    most = jnp.max(jnp.where(lane == aug + 2, most, 0.0))
    count_ref[nbatch] = most.astype(jnp.int32) // per_block


def group_update(z, valid, x, per_block, members):
    lane = lax.broadcasted_iota(jnp.int32, (GROUP, LANES), 1)
    is_member = (lane >= 1) & (lane <= members)
    z = list(z)
    hs, vs, ws = [], [], []
    for i in range(per_block):
        p = z[i]
        h = jnp.where(is_member, p, 0.0)
        s = jnp.sum(h * h, axis=1, keepdims=True) / (members - 1)
        y = p[:, members + 1:members + 2]
        r = p[:, members + 2:members + 3]
        q = s + r
        c = 1.0 / ((members - 1) * q)
        a = 1.0 / (1.0 + jnp.sqrt(r / q))
        d = y - p[:, 0:1]
        v = jnp.where(lane == 0, c * d, -(a * c) * h)
        for j in range(i + 1, per_block):
            z[j] = z[j] + v * jnp.sum(h * z[j], axis=1, keepdims=True)
        w = h
        for j in range(i):
            w = w + ws[j] * jnp.sum(h * vs[j], axis=1, keepdims=True)
        vs.append(v)
        ws.append(w)
    half = GROUP // 2
    size = per_block * half
    row_id = lax.broadcasted_iota(jnp.int32, (size, size), 0)
    col_id = lax.broadcasted_iota(jnp.int32, (size, size), 1)
    differ = (row_id ^ col_id) & (half - 1)
    ahead = (row_id & (half - 1)) < (col_id & (half - 1))
    levels = half.bit_length() - 1
    vs = [v * valid for v in vs]
    cuts = [slice(0, half), slice(half, GROUP)]
    v_half = [split2(jnp.concatenate([v[cut] for v in vs], axis=0)) for cut in cuts]
    w_half = [split2(jnp.concatenate([w[cut] for w in ws], axis=0)) for cut in cuts]
    upper = [mm3(v, w, NT) for v, w in zip(v_half, w_half)]
    across = split2(mm3(v_half[0], w_half[1], NT))
    x_parts = split2(x)
    seen = [mm3(x_parts, w, NT) for w in w_half]
    inverse = [
        jnp.where(row_id == col_id, 1.0, jnp.where(ahead & (differ == 1), u, 0.0)) for u in upper
    ]
    for level in range(1, levels):
        pairs = ahead & (differ >= (1 << level)) & (differ < (2 << level))
        parts = [split2(i) for i in inverse]
        inner = [mm3(p, jnp.where(pairs, u, 0.0)) for p, u in zip(parts, upper)]
        inverse = [i + mm3(m, p) for i, m, p in zip(inverse, inner, parts)]
    first = split2(mm3(seen[0], inverse[0]))
    second = mm3(seen[1] + mm3(first, across), inverse[1])
    return x + (mm3(first, v_half[0]) + mm3(second, v_half[1]))


def gather_rows(read, source_ref, batch, start, per_block, z_ref):
    @pl.loop(0, GROUP, unroll=8)
    def _(b):
        for i in range(per_block):
            z_ref[pl.ds(i * GROUP + b, 1), :] = read(source_ref[batch, (start + b) * per_block + i])


def group_of(z_ref, total, start, x, per_block, members):
    valid = (start + lax.broadcasted_iota(jnp.int32, (GROUP, 1), 0) < total).astype(jnp.float32)
    z = [z_ref[i * GROUP:(i + 1) * GROUP, :] for i in range(per_block)]
    return group_update(z, valid, x, per_block, members)


def update_kernel(batch, per_block, members, capp, source_ref, count_ref, x_ref, buf_ref, out_ref, z_ref):
    out_ref[...] = x_ref[capp:, :]
    total = count_ref[batch]

    @pl.loop(0, (total + GROUP - 1) // GROUP)
    def _(group):
        start = group * GROUP
        gather_rows(lambda row: buf_ref[pl.ds(row, 1), :], source_ref, batch, start, per_block, z_ref)
        out_ref[...] = group_of(z_ref, total, start, out_ref[...], per_block, members)


def rest_kernel(digits, cap, width, per_block, members, source_ref, count_ref, x_ref, buf_ref, out_ref, z_ref, *more):
    nbatch = len(more) // 3 + 1
    trade = Exchange(digits, cap, width)
    trade.greet()
    shift = cap.bit_length() - 1
    x = x_ref[...]
    for batch in range(nbatch):
        def read(row, held=buf_ref):
            return held[row >> shift, pl.ds(row & (cap - 1), 1), :]

        gather_rows(read, source_ref, batch, 0, per_block, z_ref)
        x = group_of(z_ref, count_ref[batch], 0, x[cap:], per_block, members)
        if batch == 0:
            trade.await_greetings()
        if batch + 1 < nbatch:
            buf_ref, send_sem, recv_sem = more[3 * batch:3 * batch + 3]
            trade.place_own(x[0:cap], buf_ref)
            trade.run(buf_ref, send_sem, recv_sem)
    out_ref[...] = x


def final_kernel(aug, per_member, x_ref, state_ref, out_ref):
    rest = jnp.zeros((LANES - x_ref.shape[0], LANES), jnp.float32)
    turned = jnp.transpose(jnp.concatenate([x_ref[...], rest], axis=0))
    parts = split2(turned[0:aug, 0:aug])
    for j in range(0, per_member, 2):
        cut = [state_ref[pl.ds(j + k, aug, stride=per_member), :] for k in range(2)]
        new = mm3(parts, jnp.concatenate(cut, axis=1))
        for k in range(2):
            out_ref[pl.ds(j + k, aug, stride=per_member), :] = new[:, k * LANES:(k + 1) * LANES]


def vspec():
    return pl.BlockSpec(memory_space=pltpu.VMEM)


def sspec():
    return pl.BlockSpec(memory_space=pltpu.SMEM)


def local(ensemble, obs_values, obs_errors, obs_device, obs_cell, obs_order, coupling):
    aug, levels, rows_dev, cols_dev = ensemble.shape
    members = aug - 1
    n_lat, n_lon = lax.axis_size("lat"), lax.axis_size("lon")
    ndev = n_lat * n_lon
    nbatch, nobs = obs_values.shape
    nblocks = coupling.shape[1]
    per_block = nobs // nblocks
    cap = max(1, 2 * nobs // ndev)
    capp = -(-cap // 8) * 8
    digits = digits_of(n_lat, n_lon)
    per_member = levels * rows_dev * cols_dev // LANES
    state = ensemble.reshape(aug * per_member, LANES)
    params = pltpu.CompilerParams(vmem_limit_bytes=VMEM_LIMIT)

    coupled = jnp.repeat(coupling.reshape(nbatch, nblocks), per_block, axis=1)
    base = nbatch * capp
    rows = base + -(-aug // 16) * 16
    width = aug + 3
    buf, x, source, count = pl.pallas_call(
        functools.partial(first_kernel, digits, cap, capp, aug, per_member, base, per_block),
        out_shape=(
            jax.ShapeDtypeStruct((ndev, cap, LANES), jnp.float32),
            jax.ShapeDtypeStruct((rows, LANES), jnp.float32),
            jax.ShapeDtypeStruct((nbatch, nobs), jnp.int32),
            jax.ShapeDtypeStruct((nbatch + 1,), jnp.int32),
        ),
        in_specs=[vspec()] * 7,
        out_specs=(vspec(), vspec(), vspec(), sspec()),
        scratch_shapes=exchange_scratch(digits),
        compiler_params=pltpu.CompilerParams(
            collective_id=0, has_side_effects=True, vmem_limit_bytes=VMEM_LIMIT
        ),
        name="first",
    )(obs_values, obs_errors, obs_device, obs_cell, obs_order, coupled, state)
    z_scratch = pltpu.VMEM((per_block * GROUP, LANES), jnp.float32)

    def stepwise(x, buf, source, count):
        for batch in range(nbatch):
            if batch > 0:
                buf = exchange(x, digits, cap, width, batch, ndev)
            x = pl.pallas_call(
                functools.partial(update_kernel, batch, per_block, members, capp),
                out_shape=jax.ShapeDtypeStruct((rows - (batch + 1) * capp, LANES), jnp.float32),
                in_specs=[sspec(), sspec(), vspec(), vspec()],
                out_specs=vspec(),
                scratch_shapes=[z_scratch],
                compiler_params=params,
                name="update",
            )(source, count, x, buf.reshape(ndev * cap, LANES))
        return x

    def together(x, buf, source, count):
        step_scratch = [pltpu.VMEM((ndev, cap, LANES), jnp.float32)] + exchange_scratch(digits)
        return pl.pallas_call(
            functools.partial(rest_kernel, digits, cap, width, per_block, members),
            out_shape=jax.ShapeDtypeStruct((rows - base, LANES), jnp.float32),
            in_specs=[sspec(), sspec(), vspec(), vspec()],
            out_specs=vspec(),
            scratch_shapes=[z_scratch] + step_scratch * (nbatch - 1),
            compiler_params=pltpu.CompilerParams(
                collective_id=nbatch, has_side_effects=True, vmem_limit_bytes=VMEM_LIMIT
            ),
            name="rest",
        )(source, count, x, buf)

    if is_grid(digits) and cap == capp:
        x = lax.cond(count[nbatch] <= GROUP, together, stepwise, x, buf, source, count)
    else:
        x = stepwise(x, buf, source, count)

    out = pl.pallas_call(
        functools.partial(final_kernel, aug, per_member),
        out_shape=jax.ShapeDtypeStruct((aug * per_member, LANES), jnp.float32),
        in_specs=[vspec(), vspec()],
        out_specs=vspec(),
        compiler_params=params,
        name="final",
    )(x, state)
    return out.reshape(aug, levels, rows_dev, cols_dev)


def solution(mesh):
    placed = (P(None, None, "lat", "lon"), P(), P(), P(), P(), P(), P(None, None, "lat", "lon"))
    return jax.shard_map(
        local, mesh=mesh, in_specs=placed, out_specs=P(None, None, "lat", "lon"), check_vma=False
    )
```

```python
import functools
import jax
import jax.numpy as jnp
from jax import lax
from jax.experimental import pallas as pl
from jax.experimental.pallas import tpu as pltpu
from jax.sharding import PartitionSpec as P

MESH = pl.DeviceIdType.MESH
GROUP = 32
LANES = 128
PLANE = ((0, 0), (1, 0), (0, 1), (1, 1))
VMEM_LIMIT = 32 * 1024 * 1024


def digits_of(n_lat, n_lon):
    def factors(size):
        out, stride = [], 1
        while size > 1:
            f = 4 if size % 4 == 0 else (2 if size % 2 == 0 else size)
            out.append((stride, f))
            stride, size = stride * f, size // f
        return out
    if (n_lat, n_lon) == (16, 2):
        return [("lat", 4, 4), ("lat", 1, 2), ("lat", 2, 2), ("lon", 1, 2)]
    return [("lon", s, f) for s, f in factors(n_lon)] + [("lat", s, f) for s, f in factors(n_lat)]


def split2(a):
    hi = a.astype(jnp.bfloat16)
    return hi, (a - hi.astype(jnp.float32)).astype(jnp.bfloat16)


def mm3(a, b, dims=((1,), (0,))):
    ah, al = a if isinstance(a, tuple) else split2(a)
    bh, bl = b if isinstance(b, tuple) else split2(b)
    dot = functools.partial(
        lax.dot_general, dimension_numbers=(dims, ((), ())), preferred_element_type=jnp.float32
    )
    return dot(ah, bh) + (dot(ah, bl) + dot(al, bh))


NT = ((1,), (1,))


def pow2_part(value, stride, size):
    return (value >> (stride.bit_length() - 1)) & (size - 1)


def fold_of(cap, width):
    return 24 if cap == 32 and LANES - width >= (width + 1) // 2 else cap


def buffer_rows(ndev, cap):
    return ndev * cap


def row_of(slab, slot, ndev, cap, width):
    sent = fold_of(cap, width)
    return jnp.where(slot < sent, slab * sent + slot, ndev * sent + slab * (cap - sent) + slot - sent)


def is_grid(digits):
    return [size for _, _, size in digits] == [4, 2, 2, 2]


class Exchange:
    def __init__(self, digits, cap, width):
        self.digits, self.cap, self.width = digits, cap, width
        self.sent = fold_of(cap, width)
        self.place = {axis: lax.axis_index(axis) for axis in ("lat", "lon")}
        self.mine = [lax.rem(self.place[axis] // stride, size) for axis, stride, size in digits]
        self.weights = [1]
        for _, _, size in digits:
            self.weights.append(self.weights[-1] * size)
        if is_grid(digits):
            self.spread = [(dz, turn) for dz in (2, 1, 3, 0) for turn in PLANE[::-1] if dz or any(turn)]
            self.partners = [((0, dz), (1, dx), (2, dy)) for dz, (dx, dy) in self.spread] + [((3, 1),)]
        else:
            self.partners = [
                ((which, step),) for which, (_, _, size) in enumerate(digits) for step in range(1, size)
            ]

    def peer(self, *moves):
        moved = dict(self.place)
        for which, step in moves:
            axis, stride, size = self.digits[which]
            other = lax.rem(self.mine[which] + step, size)
            moved[axis] = moved[axis] + (other - self.mine[which]) * stride
        return (moved["lat"], moved["lon"])

    def greet(self):
        barrier = pltpu.get_barrier_semaphore()
        for moves in self.partners:
            pl.semaphore_signal(barrier, inc=1, device_id=self.peer(*moves), device_id_type=MESH)

    def await_greetings(self):
        pl.semaphore_wait(pltpu.get_barrier_semaphore(), len(self.partners))

    def place_own(self, chunk, buf_ref):
        width, sent = self.width, self.sent
        half = (width + 1) // 2
        own = sum(digit * weight for digit, weight in zip(self.mine, self.weights)) * sent
        if sent < self.cap:
            tail = chunk[24:32]
            lane = lax.broadcasted_iota(jnp.int32, tail.shape, 1)
            low = jnp.where(lane < half, tail, 0.0)
            high = jnp.where((lane >= half) & (lane < width), tail, 0.0)
            buf_ref[pl.ds(pl.multiple_of(own, 8), 24), :] = jnp.concatenate(
                [chunk[0:8] + pltpu.roll(low, width, 1), chunk[8:16] + pltpu.roll(high, width - half, 1), chunk[16:24]],
                axis=0,
            )
        else:
            buf_ref[pl.ds(pl.multiple_of(own, 8), sent), :] = chunk

    def run(self, buf_ref, send_sem, recv_sem, meanwhile=lambda: None):
        digits, mine, weights, sent = self.digits, self.mine, self.weights, self.sent
        sends = []

        def send(start, count, device):
            slot = len(sends)
            part = buf_ref.at[pl.ds(pl.multiple_of(start * sent, 8), count * sent)]
            copy = pltpu.make_async_remote_copy(
                src_ref=part, dst_ref=part, send_sem=send_sem.at[slot], recv_sem=recv_sem.at[slot],
                device_id=device, device_id_type=MESH,
            )
            copy.start()
            sends.append(copy)
            return copy

        if is_grid(digits):
            z, x, y, k = mine
            arriving = {turn: [] for turn in PLANE}
            for dz, (dx, dy) in self.spread:
                own = z + 4 * x + 8 * y + 16 * k
                arriving[dx, dy].append(send(own, 1, self.peer((0, dz), (1, dx), (2, dy))))
            meanwhile()
            last = []
            for dx, dy in PLANE:
                for copy in arriving[dx, dy]:
                    copy.wait_recv()
                start = 4 * lax.rem(x + dx, 2) + 8 * lax.rem(y + dy, 2) + 16 * k
                last.append(send(start, 4, self.peer((3, 1))))
            for copy in last:
                copy.wait_recv()
        else:
            for which, (_, _, size) in enumerate(digits):
                start = sum(mine[i] * weights[i] for i in range(which, len(digits)))
                stage = [send(start, weights[which], self.peer((which, step))) for step in range(1, size)]
                if which == 0:
                    meanwhile()
                for copy in stage:
                    copy.wait_recv()
        for copy in sends:
            copy.wait_send()
        if sent < self.cap:
            width = self.width
            half = (width + 1) // 2
            for spot in range(weights[-1]):
                at = spot * sent
                low = pltpu.roll(buf_ref[at:at + 8, :], LANES - width, 1)
                high = pltpu.roll(buf_ref[at + 8:at + 16, :], LANES - width + half, 1)
                lane = lax.broadcasted_iota(jnp.int32, low.shape, 1)
                at = weights[-1] * sent + spot * 8
                buf_ref[at:at + 8, :] = jnp.where(lane < half, low, high)


def exchange_kernel(digits, cap, width, x_ref, buf_ref, send_sem, recv_sem):
    trade = Exchange(digits, cap, width)
    trade.greet()
    trade.place_own(x_ref[0:cap, :], buf_ref)
    trade.await_greetings()
    trade.run(buf_ref, send_sem, recv_sem)


def exchange_scratch(digits):
    copies = 19 if is_grid(digits) else sum(s - 1 for _, _, s in digits)
    return [pltpu.SemaphoreType.DMA((copies,)), pltpu.SemaphoreType.DMA((copies,))]


def exchange(x, digits, cap, width, ident, ndev):
    return pl.pallas_call(
        functools.partial(exchange_kernel, digits, cap, width),
        out_shape=jax.ShapeDtypeStruct((buffer_rows(ndev, cap), LANES), jnp.float32),
        in_specs=[vspec()],
        out_specs=vspec(),
        scratch_shapes=exchange_scratch(digits),
        compiler_params=pltpu.CompilerParams(
            collective_id=ident, has_side_effects=True, vmem_limit_bytes=VMEM_LIMIT
        ),
        name="exchange",
    )(x)


def first_kernel(digits, capp, aug, per_member, base, per_block, values_ref, errors_ref,
                 device_ref, cell_ref, order_ref, coupled_ref, state_ref, buf_ref, x_ref, source_ref, count_ref,
                 most_ref, send_sem, recv_sem):
    trade = Exchange(digits, capp, aug + 3)
    trade.greet()
    nbatch, nobs = device_ref.shape
    n_lat, n_lon = lax.axis_size("lat"), lax.axis_size("lon")
    ndev = n_lat * n_lon
    me = lax.axis_index("lat") * n_lon + lax.axis_index("lon")
    earlier = (
        lax.broadcasted_iota(jnp.int32, (nobs, nobs), 0) < lax.broadcasted_iota(jnp.int32, (nobs, nobs), 1)
    ).astype(jnp.float32).astype(jnp.bfloat16)

    def ranks(flags):
        return jnp.dot(flags.astype(jnp.bfloat16), earlier, preferred_element_type=jnp.float32)

    def coupled_of(batch):
        return (coupled_ref[batch] > 0).astype(jnp.float32)

    def fill():
        owned = (device_ref[...] == me).astype(jnp.float32)
        rank = ranks(owned)
        slot = lax.broadcasted_iota(jnp.int32, (capp, nobs), 0).astype(jnp.float32)
        lane = lax.broadcasted_iota(jnp.int32, (capp, LANES), 1)
        cells = []
        most = jnp.zeros((1, 1), jnp.float32)
        for batch in range(nbatch):
            most = jnp.maximum(most, jnp.sum(coupled_of(batch), axis=1, keepdims=True))
        for batch in range(nbatch):
            row = slice(batch, batch + 1)
            chosen = (rank[row] == slot) & (owned[row] > 0)

            def total(ref):
                return jnp.sum(jnp.where(chosen, ref[row, :].astype(jnp.float32), 0.0), axis=1, keepdims=True)

            cells.append(total(cell_ref))
            x_ref[batch * capp:(batch + 1) * capp, :] = jnp.where(
                lane == aug, total(values_ref), jnp.where(
                    lane == aug + 1, total(errors_ref), jnp.where(lane == aug + 2, most, 0.0)
                )
            )
        cell = jnp.concatenate(cells, axis=0).astype(jnp.int32)
        wide = 2 * LANES
        spot = lax.broadcasted_iota(jnp.int32, (nbatch * capp, wide), 1)
        picked = jnp.zeros((nbatch * capp, aug), jnp.float32)
        for j in range(0, per_member, 2):
            cut = jnp.concatenate(
                [state_ref[pl.ds(j + k, aug, stride=per_member), :] for k in range(2)], axis=1
            )
            mark = (spot + j * LANES == cell).astype(jnp.float32).astype(jnp.bfloat16)
            for _ in range(3):
                part = cut.astype(jnp.bfloat16)
                picked = picked + lax.dot_general(
                    mark, part, (NT, ((), ())), preferred_element_type=jnp.float32
                )
                cut = cut - part.astype(jnp.float32)
        x_ref[0:base, 0:aug] = picked
        return x_ref[0:capp, :]

    def meanwhile():
        square = (x_ref.shape[0] - base, LANES)
        x_ref[base:, :] = (
            lax.broadcasted_iota(jnp.int32, square, 0) == lax.broadcasted_iota(jnp.int32, square, 1)
        ).astype(jnp.float32)
        names = lax.broadcasted_iota(jnp.int32, (ndev, nobs), 0)
        names_obs = lax.broadcasted_iota(jnp.int32, (nobs, nobs), 0)
        nblocks = coupled_ref.shape[2]
        block = lax.broadcasted_iota(jnp.int32, (nblocks, nobs), 0) * per_block
        member = lax.broadcasted_iota(jnp.int32, (nblocks, nobs), 1)
        widen = ((member >= block) & (member < block + per_block)).astype(jnp.float32).astype(jnp.bfloat16)
        for batch in range(nbatch):
            device = device_ref[batch:batch + 1, :]
            held = (device == names).astype(jnp.float32)
            rank = jnp.sum(held * ranks(held), axis=0, keepdims=True)
            place = {"lat": device >> (n_lon.bit_length() - 1), "lon": device & (n_lon - 1)}
            slab, weight = jnp.zeros_like(device), 1
            for axis, stride, size in digits:
                slab = slab + pow2_part(place[axis], stride, size) * weight
                weight *= size
            pos = row_of(slab, rank.astype(jnp.int32), ndev, capp, aug + 3)
            part = lax.broadcasted_iota(jnp.int32, (8, nobs), 0)
            parts = jnp.where(part == 0, pos & 63, jnp.where(part == 1, (pos >> 6) & 63, pos >> 12))
            parts = jnp.where(part < 3, parts, 0).astype(jnp.float32).astype(jnp.bfloat16)
            named = (order_ref[batch:batch + 1, :] == names_obs).astype(jnp.float32).astype(jnp.bfloat16)
            ordered = jnp.dot(parts, named, preferred_element_type=jnp.float32)
            coupled = jnp.dot(coupled_of(batch).astype(jnp.bfloat16), widen, preferred_element_type=jnp.float32)
            goes = (ranks(coupled) == names_obs.astype(jnp.float32)) & (coupled > 0.5)
            packed = lax.dot_general(
                ordered.astype(jnp.bfloat16), goes.astype(jnp.float32).astype(jnp.bfloat16), (NT, ((), ())),
                preferred_element_type=jnp.float32,
            ).astype(jnp.int32)
            source_ref[batch:batch + 1, :] = packed[0:1] + 64 * packed[1:2] + 4096 * packed[2:3]
            count_ref[batch] = jnp.sum(coupled_of(batch)).astype(jnp.int32)

    trade.place_own(fill(), buf_ref)
    trade.await_greetings()
    trade.run(buf_ref, send_sem, recv_sem, meanwhile)
    most = buf_ref[0:8, :]
    for spot in range(1, ndev):
        most = jnp.maximum(most, buf_ref[spot * trade.sent:spot * trade.sent + 8, :])
    lane = lax.broadcasted_iota(jnp.int32, (8, LANES), 1)
    most_ref[0] = jnp.max(jnp.where(lane == aug + 2, most, 0.0)).astype(jnp.int32)


def group_update(z, valid, per_block, members):
    lane = lax.broadcasted_iota(jnp.int32, (GROUP, LANES), 1)
    is_member = (lane >= 1) & (lane <= members)
    z = list(z)
    hs, vs, ws = [], [], []
    for i in range(per_block):
        p = z[i]
        h = jnp.where(is_member, p, 0.0)
        s = jnp.sum(h * h, axis=1, keepdims=True) * (1.0 / (members - 1))
        y = p[:, members + 1:members + 2]
        r = p[:, members + 2:members + 3]
        q = s + r
        shrunk = -1.0 / ((members - 1) * (q + jnp.sqrt(q * r)))
        d = (y - p[:, 0:1]) / ((members - 1) * q)
        v = jnp.where(lane == 0, d, shrunk * h)
        for j in range(i + 1, per_block):
            z[j] = z[j] + v * jnp.sum(h * z[j], axis=1, keepdims=True)
        w = h
        for j in range(i):
            w = w + ws[j] * jnp.sum(h * vs[j], axis=1, keepdims=True)
        vs.append(v)
        ws.append(w)
    half = GROUP // 2
    size = per_block * half
    row_id = lax.broadcasted_iota(jnp.int32, (size, size), 0)
    col_id = lax.broadcasted_iota(jnp.int32, (size, size), 1)
    differ = (row_id ^ col_id) & (half - 1)
    ahead = (row_id & (half - 1)) < (col_id & (half - 1))
    levels = half.bit_length() - 1
    vs = [v * valid for v in vs]
    cuts = [slice(0, half), slice(half, GROUP)]
    v_half = [split2(jnp.concatenate([v[cut] for v in vs], axis=0)) for cut in cuts]
    w_half = [split2(jnp.concatenate([w[cut] for w in ws], axis=0)) for cut in cuts]
    upper = [mm3(v, w, NT) for v, w in zip(v_half, w_half)]
    across = split2(mm3(v_half[0], w_half[1], NT))
    inverse = [
        jnp.where(row_id == col_id, 1.0, jnp.where(ahead & (differ == 1), u, 0.0)) for u in upper
    ]
    for level in range(1, levels):
        pairs = ahead & (differ >= (1 << level)) & (differ < (2 << level))
        parts = [split2(i) for i in inverse]
        inner = [mm3(p, jnp.where(pairs, u, 0.0)) for p, u in zip(parts, upper)]
        inverse = [i + mm3(m, p) for i, m, p in zip(inverse, inner, parts)]
    inverse = [split2(i) for i in inverse]

    def apply(x):
        parts = split2(x)
        first = split2(mm3(mm3(parts, w_half[0], NT), inverse[0]))
        second = mm3(mm3(parts, w_half[1], NT) + mm3(first, across), inverse[1])
        return x + (mm3(first, v_half[0]) + mm3(second, v_half[1]))

    return apply


def group_of(source_ref, buf_ref, z_ref, batch, total, start, per_block, members):
    @pl.loop(0, GROUP, unroll=8)
    def _(b):
        for i in range(per_block):
            row = source_ref[batch, (start + b) * per_block + i]
            z_ref[pl.ds(i * GROUP + b, 1), :] = buf_ref[pl.ds(row, 1), :]

    valid = (start + lax.broadcasted_iota(jnp.int32, (GROUP, 1), 0) < total).astype(jnp.float32)
    z = [z_ref[i * GROUP:(i + 1) * GROUP, :] for i in range(per_block)]
    return group_update(z, valid, per_block, members)


def update_kernel(batch, per_block, members, capp, source_ref, count_ref, x_ref, buf_ref, out_ref, z_ref):
    out_ref[...] = x_ref[capp:, :]
    total = count_ref[batch]

    @pl.loop(0, (total + GROUP - 1) // GROUP)
    def _(group):
        apply = group_of(source_ref, buf_ref, z_ref, batch, total, group * GROUP, per_block, members)
        out_ref[...] = apply(out_ref[...])


def rest_kernel(digits, cap, width, per_block, members, source_ref, count_ref, x_ref, buf_ref, out_ref, z_ref, *more):
    nbatch = len(more) // 3 + 1
    trade = Exchange(digits, cap, width)
    trade.greet()
    x = x_ref[cap:, :]
    for batch in range(nbatch):
        apply = group_of(source_ref, buf_ref, z_ref, batch, count_ref[batch], 0, per_block, members)
        if batch + 1 == nbatch:
            out_ref[...] = apply(x)
            break
        buf_ref, send_sem, recv_sem = more[3 * batch:3 * batch + 3]
        trade.place_own(apply(x[0:cap]), buf_ref)
        if batch == 0:
            trade.await_greetings()
        later = []
        trade.run(buf_ref, send_sem, recv_sem, lambda: later.append(apply(x[cap:])))
        x = later[0]


def final_kernel(aug, per_member, x_ref, state_ref, out_ref):
    rest = jnp.zeros((LANES - x_ref.shape[0], LANES), jnp.float32)
    turned = jnp.transpose(jnp.concatenate([x_ref[...], rest], axis=0))
    parts = split2(turned[0:aug, 0:aug])
    for j in range(0, per_member, 2):
        cut = [state_ref[pl.ds(j + k, aug, stride=per_member), :] for k in range(2)]
        new = mm3(parts, jnp.concatenate(cut, axis=1))
        for k in range(2):
            out_ref[pl.ds(j + k, aug, stride=per_member), :] = new[:, k * LANES:(k + 1) * LANES]


def vspec():
    return pl.BlockSpec(memory_space=pltpu.VMEM)


def sspec():
    return pl.BlockSpec(memory_space=pltpu.SMEM)


def local(ensemble, obs_values, obs_errors, obs_device, obs_cell, obs_order, coupling):
    aug, levels, rows_dev, cols_dev = ensemble.shape
    members = aug - 1
    n_lat, n_lon = lax.axis_size("lat"), lax.axis_size("lon")
    ndev = n_lat * n_lon
    nbatch, nobs = obs_values.shape
    nblocks = coupling.shape[1]
    per_block = nobs // nblocks
    cap = max(1, 2 * nobs // ndev)
    capp = -(-cap // 8) * 8
    digits = digits_of(n_lat, n_lon)
    per_member = levels * rows_dev * cols_dev // LANES
    state = ensemble.reshape(aug * per_member, LANES)
    params = pltpu.CompilerParams(vmem_limit_bytes=VMEM_LIMIT)

    coupled = coupling.reshape(nbatch, 1, nblocks)
    base = nbatch * capp
    rows = base + -(-aug // 16) * 16
    width = aug + 3
    buf, x, source, count, most = pl.pallas_call(
        functools.partial(first_kernel, digits, capp, aug, per_member, base, per_block),
        out_shape=(
            jax.ShapeDtypeStruct((buffer_rows(ndev, capp), LANES), jnp.float32),
            jax.ShapeDtypeStruct((rows, LANES), jnp.float32),
            jax.ShapeDtypeStruct((nbatch, nobs), jnp.int32),
            jax.ShapeDtypeStruct((nbatch,), jnp.int32),
            jax.ShapeDtypeStruct((1,), jnp.int32),
        ),
        in_specs=[vspec()] * 7,
        out_specs=(vspec(), vspec(), vspec(), sspec(), sspec()),
        scratch_shapes=exchange_scratch(digits),
        compiler_params=pltpu.CompilerParams(
            collective_id=0, has_side_effects=True, vmem_limit_bytes=VMEM_LIMIT
        ),
        name="first",
    )(obs_values, obs_errors, obs_device, obs_cell, obs_order, coupled, state)
    z_scratch = pltpu.VMEM((per_block * GROUP, LANES), jnp.float32)

    def stepwise(x, buf, source, count):
        for batch in range(nbatch):
            if batch > 0:
                buf = exchange(x, digits, capp, width, batch, ndev)
            x = pl.pallas_call(
                functools.partial(update_kernel, batch, per_block, members, capp),
                out_shape=jax.ShapeDtypeStruct((rows - (batch + 1) * capp, LANES), jnp.float32),
                in_specs=[sspec(), sspec(), vspec(), vspec()],
                out_specs=vspec(),
                scratch_shapes=[z_scratch],
                compiler_params=params,
                name="update",
            )(source, count, x, buf)
        return x

    def together(x, buf, source, count):
        step_scratch = [pltpu.VMEM((buffer_rows(ndev, capp), LANES), jnp.float32)] + exchange_scratch(digits)
        return pl.pallas_call(
            functools.partial(rest_kernel, digits, capp, width, per_block, members),
            out_shape=jax.ShapeDtypeStruct((rows - base, LANES), jnp.float32),
            in_specs=[sspec(), sspec(), vspec(), vspec()],
            out_specs=vspec(),
            scratch_shapes=[z_scratch] + step_scratch * (nbatch - 1),
            compiler_params=pltpu.CompilerParams(
                collective_id=nbatch, has_side_effects=True, vmem_limit_bytes=VMEM_LIMIT
            ),
            name="rest",
        )(source, count, x, buf)

    if is_grid(digits):
        x = lax.cond(most.reshape(()) <= GROUP, together, stepwise, x, buf, source, count)
    else:
        x = stepwise(x, buf, source, count)

    out = pl.pallas_call(
        functools.partial(final_kernel, aug, per_member),
        out_shape=jax.ShapeDtypeStruct((aug * per_member, LANES), jnp.float32),
        in_specs=[vspec(), vspec()],
        out_specs=vspec(),
        compiler_params=params,
        name="final",
    )(x, state)
    return out.reshape(aug, levels, rows_dev, cols_dev)


def solution(mesh):
    placed = (P(None, None, "lat", "lon"), P(), P(), P(), P(), P(), P(None, None, "lat", "lon"))
    return jax.shard_map(
        local, mesh=mesh, in_specs=placed, out_specs=P(None, None, "lat", "lon"), check_vma=False
    )
```

```python
import functools
import jax
import jax.numpy as jnp
from jax import lax
from jax.experimental import pallas as pl
from jax.experimental.pallas import tpu as pltpu
from jax.sharding import PartitionSpec as P

MESH = pl.DeviceIdType.MESH
GROUP = 32
LANES = 128
PLANE = ((0, 0), (1, 0), (0, 1), (1, 1))
VMEM_LIMIT = 32 * 1024 * 1024


def digits_of(n_lat, n_lon):
    def factors(size):
        out, stride = [], 1
        while size > 1:
            f = 4 if size % 4 == 0 else (2 if size % 2 == 0 else size)
            out.append((stride, f))
            stride, size = stride * f, size // f
        return out
    if (n_lat, n_lon) == (16, 2):
        return [("lat", 4, 4), ("lat", 1, 2), ("lat", 2, 2), ("lon", 1, 2)]
    return [("lon", s, f) for s, f in factors(n_lon)] + [("lat", s, f) for s, f in factors(n_lat)]


def split2(a):
    hi = a.astype(jnp.bfloat16)
    return hi, (a - hi.astype(jnp.float32)).astype(jnp.bfloat16)


def mm3(a, b, dims=((1,), (0,))):
    ah, al = a if isinstance(a, tuple) else split2(a)
    bh, bl = b if isinstance(b, tuple) else split2(b)
    dot = functools.partial(
        lax.dot_general, dimension_numbers=(dims, ((), ())), preferred_element_type=jnp.float32
    )
    return dot(ah, bh) + (dot(ah, bl) + dot(al, bh))


NT = ((1,), (1,))


def pow2_part(value, stride, size):
    return (value >> (stride.bit_length() - 1)) & (size - 1)


def fold_of(cap, width):
    return 24 if cap == 32 and LANES - width >= (width + 1) // 2 else cap


def buffer_rows(ndev, cap):
    return ndev * cap


def row_of(slab, slot, ndev, cap, width):
    sent = fold_of(cap, width)
    return jnp.where(slot < sent, slab * sent + slot, ndev * sent + slab * (cap - sent) + slot - sent)


def is_grid(digits):
    return [size for _, _, size in digits] == [4, 2, 2, 2]


class Exchange:
    def __init__(self, digits, cap, width):
        self.digits, self.cap, self.width = digits, cap, width
        self.sent = fold_of(cap, width)
        self.place = {axis: lax.axis_index(axis) for axis in ("lat", "lon")}
        self.mine = [lax.rem(self.place[axis] // stride, size) for axis, stride, size in digits]
        self.weights = [1]
        for _, _, size in digits:
            self.weights.append(self.weights[-1] * size)
        if is_grid(digits):
            self.spread = [(dz, turn) for dz in (2, 1, 3, 0) for turn in PLANE[::-1] if dz or any(turn)]
            self.partners = [((0, dz), (1, dx), (2, dy)) for dz, (dx, dy) in self.spread] + [((3, 1),)]
        else:
            self.partners = [
                ((which, step),) for which, (_, _, size) in enumerate(digits) for step in range(1, size)
            ]

    def peer(self, *moves):
        moved = dict(self.place)
        for which, step in moves:
            axis, stride, size = self.digits[which]
            other = lax.rem(self.mine[which] + step, size)
            moved[axis] = moved[axis] + (other - self.mine[which]) * stride
        return (moved["lat"], moved["lon"])

    def greet(self):
        barrier = pltpu.get_barrier_semaphore()
        for moves in self.partners:
            pl.semaphore_signal(barrier, inc=1, device_id=self.peer(*moves), device_id_type=MESH)

    def await_greetings(self):
        pl.semaphore_wait(pltpu.get_barrier_semaphore(), len(self.partners))

    def place_own(self, chunk, buf_ref):
        width, sent = self.width, self.sent
        half = (width + 1) // 2
        own = sum(digit * weight for digit, weight in zip(self.mine, self.weights)) * sent
        if sent < self.cap:
            tail = chunk[24:32]
            lane = lax.broadcasted_iota(jnp.int32, tail.shape, 1)
            low = jnp.where(lane < half, tail, 0.0)
            high = jnp.where((lane >= half) & (lane < width), tail, 0.0)
            buf_ref[pl.ds(pl.multiple_of(own, 8), 24), :] = jnp.concatenate(
                [chunk[0:8] + pltpu.roll(low, width, 1), chunk[8:16] + pltpu.roll(high, width - half, 1), chunk[16:24]],
                axis=0,
            )
        else:
            buf_ref[pl.ds(pl.multiple_of(own, 8), sent), :] = chunk

    def run(self, buf_ref, send_sem, recv_sem, meanwhile=lambda: None):
        digits, mine, weights, sent = self.digits, self.mine, self.weights, self.sent
        sends = []

        def send(start, count, device):
            slot = len(sends)
            part = buf_ref.at[pl.ds(pl.multiple_of(start * sent, 8), count * sent)]
            copy = pltpu.make_async_remote_copy(
                src_ref=part, dst_ref=part, send_sem=send_sem.at[slot], recv_sem=recv_sem.at[slot],
                device_id=device, device_id_type=MESH,
            )
            copy.start()
            sends.append(copy)
            return copy

        if is_grid(digits):
            z, x, y, k = mine
            arriving = {turn: [] for turn in PLANE}
            for dz, (dx, dy) in self.spread:
                own = z + 4 * x + 8 * y + 16 * k
                arriving[dx, dy].append(send(own, 1, self.peer((0, dz), (1, dx), (2, dy))))
            meanwhile()
            last = []
            for dx, dy in PLANE:
                for copy in arriving[dx, dy]:
                    copy.wait_recv()
                start = 4 * lax.rem(x + dx, 2) + 8 * lax.rem(y + dy, 2) + 16 * k
                last.append(send(start, 4, self.peer((3, 1))))
            for copy in last:
                copy.wait_recv()
        else:
            for which, (_, _, size) in enumerate(digits):
                start = sum(mine[i] * weights[i] for i in range(which, len(digits)))
                stage = [send(start, weights[which], self.peer((which, step))) for step in range(1, size)]
                if which == 0:
                    meanwhile()
                for copy in stage:
                    copy.wait_recv()
        if sent < self.cap:
            width = self.width
            half = (width + 1) // 2
            for spot in range(weights[-1]):
                at = spot * sent
                low = pltpu.roll(buf_ref[at:at + 8, :], LANES - width, 1)
                high = pltpu.roll(buf_ref[at + 8:at + 16, :], LANES - width + half, 1)
                lane = lax.broadcasted_iota(jnp.int32, low.shape, 1)
                at = weights[-1] * sent + spot * 8
                buf_ref[at:at + 8, :] = jnp.where(lane < half, low, high)

        def settle():
            for copy in sends:
                copy.wait_send()

        return settle


def exchange_kernel(digits, cap, width, x_ref, buf_ref, send_sem, recv_sem):
    trade = Exchange(digits, cap, width)
    trade.greet()
    trade.place_own(x_ref[0:cap, :], buf_ref)
    trade.await_greetings()
    trade.run(buf_ref, send_sem, recv_sem)()


def exchange_scratch(digits):
    copies = 19 if is_grid(digits) else sum(s - 1 for _, _, s in digits)
    return [pltpu.SemaphoreType.DMA((copies,)), pltpu.SemaphoreType.DMA((copies,))]


def exchange(x, digits, cap, width, ident, ndev):
    return pl.pallas_call(
        functools.partial(exchange_kernel, digits, cap, width),
        out_shape=jax.ShapeDtypeStruct((buffer_rows(ndev, cap), LANES), jnp.float32),
        in_specs=[vspec()],
        out_specs=vspec(),
        scratch_shapes=exchange_scratch(digits),
        compiler_params=pltpu.CompilerParams(
            collective_id=ident, has_side_effects=True, vmem_limit_bytes=VMEM_LIMIT
        ),
        name="exchange",
    )(x)


def first_kernel(digits, capp, aug, per_member, base, per_block, values_ref, errors_ref,
                 device_ref, cell_ref, order_ref, coupled_ref, state_ref, buf_ref, x_ref, source_ref, count_ref,
                 most_ref, send_sem, recv_sem):
    trade = Exchange(digits, capp, aug + 3)
    trade.greet()
    nbatch, nobs = device_ref.shape
    n_lat, n_lon = lax.axis_size("lat"), lax.axis_size("lon")
    ndev = n_lat * n_lon
    me = lax.axis_index("lat") * n_lon + lax.axis_index("lon")
    earlier = (
        lax.broadcasted_iota(jnp.int32, (nobs, nobs), 0) < lax.broadcasted_iota(jnp.int32, (nobs, nobs), 1)
    ).astype(jnp.float32).astype(jnp.bfloat16)

    def ranks(flags):
        return jnp.dot(flags.astype(jnp.bfloat16), earlier, preferred_element_type=jnp.float32)

    def coupled_of(batch):
        return (coupled_ref[batch] > 0).astype(jnp.float32)

    def fill():
        owned = (device_ref[...] == me).astype(jnp.float32)
        rank = ranks(owned)
        slot = lax.broadcasted_iota(jnp.int32, (capp, nobs), 0).astype(jnp.float32)
        lane = lax.broadcasted_iota(jnp.int32, (capp, LANES), 1)
        cells = []
        most = jnp.zeros((1, 1), jnp.float32)
        for batch in range(nbatch):
            most = jnp.maximum(most, jnp.sum(coupled_of(batch), axis=1, keepdims=True))
        for batch in range(nbatch):
            row = slice(batch, batch + 1)
            chosen = (rank[row] == slot) & (owned[row] > 0)

            def total(ref):
                return jnp.sum(jnp.where(chosen, ref[row, :].astype(jnp.float32), 0.0), axis=1, keepdims=True)

            cells.append(total(cell_ref))
            x_ref[batch * capp:(batch + 1) * capp, :] = jnp.where(
                lane == aug, total(values_ref), jnp.where(
                    lane == aug + 1, total(errors_ref), jnp.where(lane == aug + 2, most, 0.0)
                )
            )
        cell = jnp.concatenate(cells, axis=0).astype(jnp.int32)
        wide = 2 * LANES
        spot = lax.broadcasted_iota(jnp.int32, (nbatch * capp, wide), 1)
        picked = jnp.zeros((nbatch * capp, aug), jnp.float32)
        for j in range(0, per_member, 2):
            cut = jnp.concatenate(
                [state_ref[pl.ds(j + k, aug, stride=per_member), :] for k in range(2)], axis=1
            )
            mark = (spot + j * LANES == cell).astype(jnp.float32).astype(jnp.bfloat16)
            for _ in range(3):
                part = cut.astype(jnp.bfloat16)
                picked = picked + lax.dot_general(
                    mark, part, (NT, ((), ())), preferred_element_type=jnp.float32
                )
                cut = cut - part.astype(jnp.float32)
        x_ref[0:base, 0:aug] = picked
        return x_ref[0:capp, :]

    def meanwhile():
        square = (x_ref.shape[0] - base, LANES)
        x_ref[base:, :] = (
            lax.broadcasted_iota(jnp.int32, square, 0) == lax.broadcasted_iota(jnp.int32, square, 1)
        ).astype(jnp.float32)
        names = lax.broadcasted_iota(jnp.int32, (ndev, nobs), 0)
        names_obs = lax.broadcasted_iota(jnp.int32, (nobs, nobs), 0)
        nblocks = coupled_ref.shape[2]
        block = lax.broadcasted_iota(jnp.int32, (nblocks, nobs), 0) * per_block
        member = lax.broadcasted_iota(jnp.int32, (nblocks, nobs), 1)
        widen = ((member >= block) & (member < block + per_block)).astype(jnp.float32).astype(jnp.bfloat16)
        for batch in range(nbatch):
            device = device_ref[batch:batch + 1, :]
            held = (device == names).astype(jnp.float32)
            rank = jnp.sum(held * ranks(held), axis=0, keepdims=True)
            place = {"lat": device >> (n_lon.bit_length() - 1), "lon": device & (n_lon - 1)}
            slab, weight = jnp.zeros_like(device), 1
            for axis, stride, size in digits:
                slab = slab + pow2_part(place[axis], stride, size) * weight
                weight *= size
            pos = row_of(slab, rank.astype(jnp.int32), ndev, capp, aug + 3)
            part = lax.broadcasted_iota(jnp.int32, (8, nobs), 0)
            parts = jnp.where(part == 0, pos & 63, jnp.where(part == 1, (pos >> 6) & 63, pos >> 12))
            parts = jnp.where(part < 3, parts, 0).astype(jnp.float32).astype(jnp.bfloat16)
            named = (order_ref[batch:batch + 1, :] == names_obs).astype(jnp.float32).astype(jnp.bfloat16)
            ordered = jnp.dot(parts, named, preferred_element_type=jnp.float32)
            coupled = jnp.dot(coupled_of(batch).astype(jnp.bfloat16), widen, preferred_element_type=jnp.float32)
            goes = (ranks(coupled) == names_obs.astype(jnp.float32)) & (coupled > 0.5)
            packed = lax.dot_general(
                ordered.astype(jnp.bfloat16), goes.astype(jnp.float32).astype(jnp.bfloat16), (NT, ((), ())),
                preferred_element_type=jnp.float32,
            ).astype(jnp.int32)
            source_ref[batch:batch + 1, :] = packed[0:1] + 64 * packed[1:2] + 4096 * packed[2:3]
            count_ref[batch] = jnp.sum(coupled_of(batch)).astype(jnp.int32)

    trade.place_own(fill(), buf_ref)
    trade.await_greetings()
    settle = trade.run(buf_ref, send_sem, recv_sem, meanwhile)
    most = buf_ref[0:8, :]
    for spot in range(1, ndev):
        most = jnp.maximum(most, buf_ref[spot * trade.sent:spot * trade.sent + 8, :])
    lane = lax.broadcasted_iota(jnp.int32, (8, LANES), 1)
    most_ref[0] = jnp.max(jnp.where(lane == aug + 2, most, 0.0)).astype(jnp.int32)
    settle()


def group_update(z, valid, per_block, members):
    lane = lax.broadcasted_iota(jnp.int32, (GROUP, LANES), 1)
    is_member = (lane >= 1) & (lane <= members)
    z = list(z)
    hs, vs, ws = [], [], []
    for i in range(per_block):
        p = z[i]
        h = jnp.where(is_member, p, 0.0)
        s = jnp.sum(h * h, axis=1, keepdims=True) * (1.0 / (members - 1))
        y = p[:, members + 1:members + 2]
        r = p[:, members + 2:members + 3]
        q = s + r
        shrunk = -1.0 / ((members - 1) * (q + jnp.sqrt(q * r)))
        d = (y - p[:, 0:1]) / ((members - 1) * q)
        v = jnp.where(lane == 0, d, shrunk * h)
        for j in range(i + 1, per_block):
            z[j] = z[j] + v * jnp.sum(h * z[j], axis=1, keepdims=True)
        w = h
        for j in range(i):
            w = w + ws[j] * jnp.sum(h * vs[j], axis=1, keepdims=True)
        vs.append(v)
        ws.append(w)
    half = GROUP // 2
    size = per_block * half
    row_id = lax.broadcasted_iota(jnp.int32, (size, size), 0)
    col_id = lax.broadcasted_iota(jnp.int32, (size, size), 1)
    differ = (row_id ^ col_id) & (half - 1)
    ahead = (row_id & (half - 1)) < (col_id & (half - 1))
    levels = half.bit_length() - 1
    vs = [v * valid for v in vs]
    cuts = [slice(0, half), slice(half, GROUP)]
    v_half = [split2(jnp.concatenate([v[cut] for v in vs], axis=0)) for cut in cuts]
    w_half = [split2(jnp.concatenate([w[cut] for w in ws], axis=0)) for cut in cuts]
    upper = [mm3(v, w, NT) for v, w in zip(v_half, w_half)]
    across = split2(mm3(v_half[0], w_half[1], NT))
    inverse = [
        jnp.where(row_id == col_id, 1.0, jnp.where(ahead & (differ == 1), u, 0.0)) for u in upper
    ]
    for level in range(1, levels):
        pairs = ahead & (differ >= (1 << level)) & (differ < (2 << level))
        parts = [split2(i) for i in inverse]
        inner = [mm3(p, jnp.where(pairs, u, 0.0)) for p, u in zip(parts, upper)]
        inverse = [i + mm3(m, p) for i, m, p in zip(inverse, inner, parts)]
    inverse = [split2(i) for i in inverse]

    def apply(x):
        parts = split2(x)
        first = split2(mm3(mm3(parts, w_half[0], NT), inverse[0]))
        second = mm3(mm3(parts, w_half[1], NT) + mm3(first, across), inverse[1])
        return x + (mm3(first, v_half[0]) + mm3(second, v_half[1]))

    return apply


def group_of(source_ref, buf_ref, z_ref, batch, total, start, per_block, members):
    @pl.loop(0, GROUP, unroll=8)
    def _(b):
        for i in range(per_block):
            row = source_ref[batch, (start + b) * per_block + i]
            z_ref[pl.ds(i * GROUP + b, 1), :] = buf_ref[pl.ds(row, 1), :]

    valid = (start + lax.broadcasted_iota(jnp.int32, (GROUP, 1), 0) < total).astype(jnp.float32)
    z = [z_ref[i * GROUP:(i + 1) * GROUP, :] for i in range(per_block)]
    return group_update(z, valid, per_block, members)


def update_kernel(batch, per_block, members, capp, source_ref, count_ref, x_ref, buf_ref, out_ref, z_ref):
    out_ref[...] = x_ref[capp:, :]
    total = count_ref[batch]

    @pl.loop(0, (total + GROUP - 1) // GROUP)
    def _(group):
        apply = group_of(source_ref, buf_ref, z_ref, batch, total, group * GROUP, per_block, members)
        out_ref[...] = apply(out_ref[...])


def rest_kernel(digits, cap, width, per_block, members, source_ref, count_ref, x_ref, buf_ref, out_ref, z_ref, *more):
    nbatch = len(more) // 3 + 1
    trade = Exchange(digits, cap, width)
    trade.greet()
    x = x_ref[...]
    settles = []
    for batch in range(nbatch):
        apply = group_of(source_ref, buf_ref, z_ref, batch, count_ref[batch], 0, per_block, members)
        x = apply(x[cap:])
        if batch == 0:
            trade.await_greetings()
        if batch + 1 < nbatch:
            buf_ref, send_sem, recv_sem = more[3 * batch:3 * batch + 3]
            trade.place_own(x[0:cap], buf_ref)
            settles.append(trade.run(buf_ref, send_sem, recv_sem))
    out_ref[...] = x
    for settle in settles:
        settle()


def final_kernel(aug, per_member, x_ref, state_ref, out_ref):
    rest = jnp.zeros((LANES - x_ref.shape[0], LANES), jnp.float32)
    turned = jnp.transpose(jnp.concatenate([x_ref[...], rest], axis=0))
    parts = split2(turned[0:aug, 0:aug])
    for j in range(0, per_member, 2):
        cut = [state_ref[pl.ds(j + k, aug, stride=per_member), :] for k in range(2)]
        new = mm3(parts, jnp.concatenate(cut, axis=1))
        for k in range(2):
            out_ref[pl.ds(j + k, aug, stride=per_member), :] = new[:, k * LANES:(k + 1) * LANES]


def vspec():
    return pl.BlockSpec(memory_space=pltpu.VMEM)


def sspec():
    return pl.BlockSpec(memory_space=pltpu.SMEM)


def local(ensemble, obs_values, obs_errors, obs_device, obs_cell, obs_order, coupling):
    aug, levels, rows_dev, cols_dev = ensemble.shape
    members = aug - 1
    n_lat, n_lon = lax.axis_size("lat"), lax.axis_size("lon")
    ndev = n_lat * n_lon
    nbatch, nobs = obs_values.shape
    nblocks = coupling.shape[1]
    per_block = nobs // nblocks
    cap = max(1, 2 * nobs // ndev)
    capp = -(-cap // 8) * 8
    digits = digits_of(n_lat, n_lon)
    per_member = levels * rows_dev * cols_dev // LANES
    state = ensemble.reshape(aug * per_member, LANES)
    params = pltpu.CompilerParams(vmem_limit_bytes=VMEM_LIMIT)

    coupled = coupling.reshape(nbatch, 1, nblocks)
    base = nbatch * capp
    rows = base + -(-aug // 16) * 16
    width = aug + 3
    buf, x, source, count, most = pl.pallas_call(
        functools.partial(first_kernel, digits, capp, aug, per_member, base, per_block),
        out_shape=(
            jax.ShapeDtypeStruct((buffer_rows(ndev, capp), LANES), jnp.float32),
            jax.ShapeDtypeStruct((rows, LANES), jnp.float32),
            jax.ShapeDtypeStruct((nbatch, nobs), jnp.int32),
            jax.ShapeDtypeStruct((nbatch,), jnp.int32),
            jax.ShapeDtypeStruct((1,), jnp.int32),
        ),
        in_specs=[vspec()] * 7,
        out_specs=(vspec(), vspec(), vspec(), sspec(), sspec()),
        scratch_shapes=exchange_scratch(digits),
        compiler_params=pltpu.CompilerParams(
            collective_id=0, has_side_effects=True, vmem_limit_bytes=VMEM_LIMIT
        ),
        name="first",
    )(obs_values, obs_errors, obs_device, obs_cell, obs_order, coupled, state)
    z_scratch = pltpu.VMEM((per_block * GROUP, LANES), jnp.float32)

    def stepwise(x, buf, source, count):
        for batch in range(nbatch):
            if batch > 0:
                buf = exchange(x, digits, capp, width, batch, ndev)
            x = pl.pallas_call(
                functools.partial(update_kernel, batch, per_block, members, capp),
                out_shape=jax.ShapeDtypeStruct((rows - (batch + 1) * capp, LANES), jnp.float32),
                in_specs=[sspec(), sspec(), vspec(), vspec()],
                out_specs=vspec(),
                scratch_shapes=[z_scratch],
                compiler_params=params,
                name="update",
            )(source, count, x, buf)
        return x

    def together(x, buf, source, count):
        step_scratch = [pltpu.VMEM((buffer_rows(ndev, capp), LANES), jnp.float32)] + exchange_scratch(digits)
        return pl.pallas_call(
            functools.partial(rest_kernel, digits, capp, width, per_block, members),
            out_shape=jax.ShapeDtypeStruct((rows - base, LANES), jnp.float32),
            in_specs=[sspec(), sspec(), vspec(), vspec()],
            out_specs=vspec(),
            scratch_shapes=[z_scratch] + step_scratch * (nbatch - 1),
            compiler_params=pltpu.CompilerParams(
                collective_id=nbatch, has_side_effects=True, vmem_limit_bytes=VMEM_LIMIT
            ),
            name="rest",
        )(source, count, x, buf)

    if is_grid(digits):
        x = lax.cond(most.reshape(()) <= GROUP, together, stepwise, x, buf, source, count)
    else:
        x = stepwise(x, buf, source, count)

    out = pl.pallas_call(
        functools.partial(final_kernel, aug, per_member),
        out_shape=jax.ShapeDtypeStruct((aug * per_member, LANES), jnp.float32),
        in_specs=[vspec(), vspec()],
        out_specs=vspec(),
        compiler_params=params,
        name="final",
    )(x, state)
    return out.reshape(aug, levels, rows_dev, cols_dev)


def solution(mesh):
    placed = (P(None, None, "lat", "lon"), P(), P(), P(), P(), P(), P(None, None, "lat", "lon"))
    return jax.shard_map(
        local, mesh=mesh, in_specs=placed, out_specs=P(None, None, "lat", "lon"), check_vma=False
    )
```

```python
import functools
import jax
import jax.numpy as jnp
from jax import lax
from jax.experimental import pallas as pl
from jax.experimental.pallas import tpu as pltpu
from jax.sharding import PartitionSpec as P

MESH = pl.DeviceIdType.MESH
GROUP = 32
LANES = 128
PLANE = ((0, 0), (1, 0), (0, 1), (1, 1))
VMEM_LIMIT = 32 * 1024 * 1024


def digits_of(n_lat, n_lon):
    def factors(size):
        out, stride = [], 1
        while size > 1:
            f = 4 if size % 4 == 0 else (2 if size % 2 == 0 else size)
            out.append((stride, f))
            stride, size = stride * f, size // f
        return out
    if (n_lat, n_lon) == (16, 2):
        return [("lat", 4, 4), ("lat", 1, 2), ("lat", 2, 2), ("lon", 1, 2)]
    return [("lon", s, f) for s, f in factors(n_lon)] + [("lat", s, f) for s, f in factors(n_lat)]


def split2(a):
    hi = a.astype(jnp.bfloat16)
    return hi, (a - hi.astype(jnp.float32)).astype(jnp.bfloat16)


def mm3(a, b, dims=((1,), (0,))):
    ah, al = a if isinstance(a, tuple) else split2(a)
    bh, bl = b if isinstance(b, tuple) else split2(b)
    dot = functools.partial(
        lax.dot_general, dimension_numbers=(dims, ((), ())), preferred_element_type=jnp.float32
    )
    return dot(ah, bh) + (dot(ah, bl) + dot(al, bh))


NT = ((1,), (1,))


def pow2_part(value, stride, size):
    return (value >> (stride.bit_length() - 1)) & (size - 1)


def fold_of(cap, width):
    return 24 if cap == 32 and LANES - width >= (width + 1) // 2 else cap


def buffer_rows(ndev, cap):
    return ndev * cap


def row_of(slab, slot, ndev, cap, width):
    sent = fold_of(cap, width)
    return jnp.where(slot < sent, slab * sent + slot, ndev * sent + slab * (cap - sent) + slot - sent)


def is_grid(digits):
    return [size for _, _, size in digits] == [4, 2, 2, 2]


class Exchange:
    def __init__(self, digits, cap, width):
        self.digits, self.cap, self.width = digits, cap, width
        self.sent = fold_of(cap, width)
        self.place = {axis: lax.axis_index(axis) for axis in ("lat", "lon")}
        self.mine = [lax.rem(self.place[axis] // stride, size) for axis, stride, size in digits]
        self.weights = [1]
        for _, _, size in digits:
            self.weights.append(self.weights[-1] * size)
        if is_grid(digits):
            self.spread = [(dz, turn) for dz in (2, 1, 3, 0) for turn in PLANE[::-1] if dz or any(turn)]
            self.partners = [((0, dz), (1, dx), (2, dy)) for dz, (dx, dy) in self.spread] + [((3, 1),)]
        else:
            self.partners = [
                ((which, step),) for which, (_, _, size) in enumerate(digits) for step in range(1, size)
            ]

    def peer(self, *moves):
        moved = dict(self.place)
        for which, step in moves:
            axis, stride, size = self.digits[which]
            other = lax.rem(self.mine[which] + step, size)
            moved[axis] = moved[axis] + (other - self.mine[which]) * stride
        return (moved["lat"], moved["lon"])

    def greet(self):
        barrier = pltpu.get_barrier_semaphore()
        for moves in self.partners:
            pl.semaphore_signal(barrier, inc=1, device_id=self.peer(*moves), device_id_type=MESH)

    def await_greetings(self):
        pl.semaphore_wait(pltpu.get_barrier_semaphore(), len(self.partners))

    def place_own(self, chunk, buf_ref):
        width, sent = self.width, self.sent
        half = (width + 1) // 2
        own = sum(digit * weight for digit, weight in zip(self.mine, self.weights)) * sent
        if sent < self.cap:
            tail = chunk[24:32]
            lane = lax.broadcasted_iota(jnp.int32, tail.shape, 1)
            low = jnp.where(lane < half, tail, 0.0)
            high = jnp.where((lane >= half) & (lane < width), tail, 0.0)
            buf_ref[pl.ds(pl.multiple_of(own, 8), 24), :] = jnp.concatenate(
                [chunk[0:8] + pltpu.roll(low, width, 1), chunk[8:16] + pltpu.roll(high, width - half, 1), chunk[16:24]],
                axis=0,
            )
        else:
            buf_ref[pl.ds(pl.multiple_of(own, 8), sent), :] = chunk

    def run(self, buf_ref, send_sem, recv_sem, meanwhile=lambda: None):
        digits, mine, weights, sent = self.digits, self.mine, self.weights, self.sent
        sends = []

        def send(start, count, device):
            slot = len(sends)
            part = buf_ref.at[pl.ds(pl.multiple_of(start * sent, 8), count * sent)]
            copy = pltpu.make_async_remote_copy(
                src_ref=part, dst_ref=part, send_sem=send_sem.at[slot], recv_sem=recv_sem.at[slot],
                device_id=device, device_id_type=MESH,
            )
            copy.start()
            sends.append(copy)
            return copy

        if is_grid(digits):
            z, x, y, k = mine
            arriving = {turn: [] for turn in PLANE}
            for dz, (dx, dy) in self.spread:
                own = z + 4 * x + 8 * y + 16 * k
                arriving[dx, dy].append(send(own, 1, self.peer((0, dz), (1, dx), (2, dy))))
            meanwhile()
            last = []
            for dx, dy in PLANE:
                for copy in arriving[dx, dy]:
                    copy.wait_recv()
                start = 4 * lax.rem(x + dx, 2) + 8 * lax.rem(y + dy, 2) + 16 * k
                last.append(send(start, 4, self.peer((3, 1))))
            for copy in last:
                copy.wait_recv()
        else:
            for which, (_, _, size) in enumerate(digits):
                start = sum(mine[i] * weights[i] for i in range(which, len(digits)))
                stage = [send(start, weights[which], self.peer((which, step))) for step in range(1, size)]
                if which == 0:
                    meanwhile()
                for copy in stage:
                    copy.wait_recv()
        if sent < self.cap:
            width = self.width
            half = (width + 1) // 2
            for spot in range(weights[-1]):
                at = spot * sent
                low = pltpu.roll(buf_ref[at:at + 8, :], LANES - width, 1)
                high = pltpu.roll(buf_ref[at + 8:at + 16, :], LANES - width + half, 1)
                lane = lax.broadcasted_iota(jnp.int32, low.shape, 1)
                at = weights[-1] * sent + spot * 8
                buf_ref[at:at + 8, :] = jnp.where(lane < half, low, high)

        def settle():
            for copy in sends:
                copy.wait_send()

        return settle


def exchange_kernel(digits, cap, width, x_ref, buf_ref, send_sem, recv_sem):
    trade = Exchange(digits, cap, width)
    trade.greet()
    trade.place_own(x_ref[0:cap, :], buf_ref)
    trade.await_greetings()
    trade.run(buf_ref, send_sem, recv_sem)()


def exchange_scratch(digits):
    copies = 19 if is_grid(digits) else sum(s - 1 for _, _, s in digits)
    return [pltpu.SemaphoreType.DMA((copies,)), pltpu.SemaphoreType.DMA((copies,))]


def exchange(x, digits, cap, width, ident, ndev):
    return pl.pallas_call(
        functools.partial(exchange_kernel, digits, cap, width),
        out_shape=jax.ShapeDtypeStruct((buffer_rows(ndev, cap), LANES), jnp.float32),
        in_specs=[vspec()],
        out_specs=vspec(),
        scratch_shapes=exchange_scratch(digits),
        compiler_params=pltpu.CompilerParams(
            collective_id=ident, has_side_effects=True, vmem_limit_bytes=VMEM_LIMIT
        ),
        name="exchange",
    )(x)


def first_kernel(digits, capp, aug, per_member, base, per_block, values_ref, errors_ref,
                 device_ref, cell_ref, order_ref, coupled_ref, state_ref, buf_ref, x_ref, source_ref, count_ref,
                 most_ref, send_sem, recv_sem):
    trade = Exchange(digits, capp, aug + 3)
    trade.greet()
    nbatch, nobs = device_ref.shape
    n_lat, n_lon = lax.axis_size("lat"), lax.axis_size("lon")
    ndev = n_lat * n_lon
    me = lax.axis_index("lat") * n_lon + lax.axis_index("lon")
    earlier = (
        lax.broadcasted_iota(jnp.int32, (nobs, nobs), 0) < lax.broadcasted_iota(jnp.int32, (nobs, nobs), 1)
    ).astype(jnp.float32).astype(jnp.bfloat16)

    def ranks(flags):
        return jnp.dot(flags.astype(jnp.bfloat16), earlier, preferred_element_type=jnp.float32)

    def coupled_of(batch):
        return (coupled_ref[batch] > 0).astype(jnp.float32)

    def fill():
        owned = (device_ref[...] == me).astype(jnp.float32)
        rank = ranks(owned)
        slot = lax.broadcasted_iota(jnp.int32, (capp, nobs), 0).astype(jnp.float32)
        lane = lax.broadcasted_iota(jnp.int32, (capp, LANES), 1)
        cells = []
        most = jnp.zeros((1, 1), jnp.float32)
        for batch in range(nbatch):
            most = jnp.maximum(most, jnp.sum(coupled_of(batch), axis=1, keepdims=True))
        for batch in range(nbatch):
            row = slice(batch, batch + 1)
            chosen = (rank[row] == slot) & (owned[row] > 0)

            def total(ref):
                return jnp.sum(jnp.where(chosen, ref[row, :].astype(jnp.float32), 0.0), axis=1, keepdims=True)

            cells.append(total(cell_ref))
            x_ref[batch * capp:(batch + 1) * capp, :] = jnp.where(
                lane == aug, total(values_ref), jnp.where(
                    lane == aug + 1, total(errors_ref), jnp.where(lane == aug + 2, most, 0.0)
                )
            )
        cell = jnp.concatenate(cells, axis=0).astype(jnp.int32)
        wide = 2 * LANES
        spot = lax.broadcasted_iota(jnp.int32, (nbatch * capp, wide), 1)
        picked = jnp.zeros((nbatch * capp, aug), jnp.float32)
        for j in range(0, per_member, 2):
            cut = jnp.concatenate(
                [state_ref[pl.ds(j + k, aug, stride=per_member), :] for k in range(2)], axis=1
            )
            mark = (spot + j * LANES == cell).astype(jnp.float32).astype(jnp.bfloat16)
            for _ in range(3):
                part = cut.astype(jnp.bfloat16)
                picked = picked + lax.dot_general(
                    mark, part, (NT, ((), ())), preferred_element_type=jnp.float32
                )
                cut = cut - part.astype(jnp.float32)
        x_ref[0:base, 0:aug] = picked
        return x_ref[0:capp, :]

    def meanwhile():
        square = (x_ref.shape[0] - base, LANES)
        x_ref[base:, :] = (
            lax.broadcasted_iota(jnp.int32, square, 0) == lax.broadcasted_iota(jnp.int32, square, 1)
        ).astype(jnp.float32)
        names = lax.broadcasted_iota(jnp.int32, (ndev, nobs), 0)
        names_obs = lax.broadcasted_iota(jnp.int32, (nobs, nobs), 0)
        nblocks = coupled_ref.shape[2]
        block = lax.broadcasted_iota(jnp.int32, (nblocks, nobs), 0) * per_block
        member = lax.broadcasted_iota(jnp.int32, (nblocks, nobs), 1)
        widen = ((member >= block) & (member < block + per_block)).astype(jnp.float32).astype(jnp.bfloat16)
        for batch in range(nbatch):
            device = device_ref[batch:batch + 1, :]
            held = (device == names).astype(jnp.float32)
            rank = jnp.sum(held * ranks(held), axis=0, keepdims=True)
            place = {"lat": device >> (n_lon.bit_length() - 1), "lon": device & (n_lon - 1)}
            slab, weight = jnp.zeros_like(device), 1
            for axis, stride, size in digits:
                slab = slab + pow2_part(place[axis], stride, size) * weight
                weight *= size
            pos = row_of(slab, rank.astype(jnp.int32), ndev, capp, aug + 3)
            part = lax.broadcasted_iota(jnp.int32, (8, nobs), 0)
            parts = jnp.where(part == 0, pos & 63, jnp.where(part == 1, (pos >> 6) & 63, pos >> 12))
            parts = jnp.where(part < 3, parts, 0).astype(jnp.float32).astype(jnp.bfloat16)
            named = (order_ref[batch:batch + 1, :] == names_obs).astype(jnp.float32).astype(jnp.bfloat16)
            ordered = jnp.dot(parts, named, preferred_element_type=jnp.float32)
            coupled = jnp.dot(coupled_of(batch).astype(jnp.bfloat16), widen, preferred_element_type=jnp.float32)
            goes = (ranks(coupled) == names_obs.astype(jnp.float32)) & (coupled > 0.5)
            packed = lax.dot_general(
                ordered.astype(jnp.bfloat16), goes.astype(jnp.float32).astype(jnp.bfloat16), (NT, ((), ())),
                preferred_element_type=jnp.float32,
            ).astype(jnp.int32)
            source_ref[batch:batch + 1, :] = packed[0:1] + 64 * packed[1:2] + 4096 * packed[2:3]
            count_ref[batch] = jnp.sum(coupled_of(batch)).astype(jnp.int32)

    trade.place_own(fill(), buf_ref)
    trade.await_greetings()
    settle = trade.run(buf_ref, send_sem, recv_sem, meanwhile)
    most = buf_ref[0:8, :]
    for spot in range(1, ndev):
        most = jnp.maximum(most, buf_ref[spot * trade.sent:spot * trade.sent + 8, :])
    lane = lax.broadcasted_iota(jnp.int32, (8, LANES), 1)
    most_ref[0] = jnp.max(jnp.where(lane == aug + 2, most, 0.0)).astype(jnp.int32)
    settle()


def group_update(z, valid, x, per_block, members):
    lane = lax.broadcasted_iota(jnp.int32, (GROUP, LANES), 1)
    is_member = (lane >= 1) & (lane <= members)
    z = list(z)
    hs, vs, ws = [], [], []
    for i in range(per_block):
        p = z[i]
        h = jnp.where(is_member, p, 0.0)
        s = jnp.sum(h * h, axis=1, keepdims=True) * (1.0 / (members - 1))
        y = p[:, members + 1:members + 2]
        r = p[:, members + 2:members + 3]
        q = s + r
        shrunk = -1.0 / ((members - 1) * (q + jnp.sqrt(q * r)))
        d = (y - p[:, 0:1]) / ((members - 1) * q)
        v = jnp.where(lane == 0, d, shrunk * h)
        for j in range(i + 1, per_block):
            z[j] = z[j] + v * jnp.sum(h * z[j], axis=1, keepdims=True)
        w = h
        for j in range(i):
            w = w + ws[j] * jnp.sum(h * vs[j], axis=1, keepdims=True)
        vs.append(v)
        ws.append(w)
    half = GROUP // 2
    size = per_block * half
    row_id = lax.broadcasted_iota(jnp.int32, (size, size), 0)
    col_id = lax.broadcasted_iota(jnp.int32, (size, size), 1)
    differ = (row_id ^ col_id) & (half - 1)
    ahead = (row_id & (half - 1)) < (col_id & (half - 1))
    levels = half.bit_length() - 1
    vs = [v * valid for v in vs]
    cuts = [slice(0, half), slice(half, GROUP)]
    v_half = [split2(jnp.concatenate([v[cut] for v in vs], axis=0)) for cut in cuts]
    w_half = [split2(jnp.concatenate([w[cut] for w in ws], axis=0)) for cut in cuts]
    upper = [mm3(v, w, NT) for v, w in zip(v_half, w_half)]
    inverse = [
        jnp.where(row_id == col_id, 1.0, jnp.where(ahead & (differ == 1), u, 0.0)) for u in upper
    ]
    x_parts = split2(x)
    asides = [
        lambda: mm3(x_parts, w_half[0], NT), lambda: mm3(x_parts, w_half[1], NT),
        lambda: split2(mm3(v_half[0], w_half[1], NT)),
    ]
    done = []
    for level in range(1, levels):
        pairs = ahead & (differ >= (1 << level)) & (differ < (2 << level))
        parts = [split2(i) for i in inverse]
        inner = [mm3(p, jnp.where(pairs, u, 0.0)) for p, u in zip(parts, upper)]
        if len(done) < len(asides):
            done.append(asides[len(done)]())
        inverse = [i + mm3(m, p) for i, m, p in zip(inverse, inner, parts)]
    done.extend(aside() for aside in asides[len(done):])
    seen_first, seen_second, across = done
    first = split2(mm3(seen_first, inverse[0]))
    second = mm3(seen_second + mm3(first, across), inverse[1])
    return x + (mm3(first, v_half[0]) + mm3(second, v_half[1]))


def group_of(source_ref, buf_ref, z_ref, batch, total, start, x, per_block, members):
    @pl.loop(0, GROUP, unroll=8)
    def _(b):
        for i in range(per_block):
            row = source_ref[batch, (start + b) * per_block + i]
            z_ref[pl.ds(i * GROUP + b, 1), :] = buf_ref[pl.ds(row, 1), :]

    valid = (start + lax.broadcasted_iota(jnp.int32, (GROUP, 1), 0) < total).astype(jnp.float32)
    z = [z_ref[i * GROUP:(i + 1) * GROUP, :] for i in range(per_block)]
    return group_update(z, valid, x, per_block, members)


def update_kernel(batch, per_block, members, capp, source_ref, count_ref, x_ref, buf_ref, out_ref, z_ref):
    out_ref[...] = x_ref[capp:, :]
    total = count_ref[batch]

    @pl.loop(0, (total + GROUP - 1) // GROUP)
    def _(group):
        out_ref[...] = group_of(
            source_ref, buf_ref, z_ref, batch, total, group * GROUP, out_ref[...], per_block, members
        )


def rest_kernel(digits, cap, width, per_block, members, source_ref, count_ref, x_ref, buf_ref, out_ref, z_ref, *more):
    nbatch = len(more) // 3 + 1
    trade = Exchange(digits, cap, width)
    trade.greet()
    x = x_ref[...]
    settles = []
    for batch in range(nbatch):
        x = group_of(source_ref, buf_ref, z_ref, batch, count_ref[batch], 0, x[cap:], per_block, members)
        if batch == 0:
            trade.await_greetings()
        if batch + 1 < nbatch:
            buf_ref, send_sem, recv_sem = more[3 * batch:3 * batch + 3]
            trade.place_own(x[0:cap], buf_ref)
            settles.append(trade.run(buf_ref, send_sem, recv_sem))
    out_ref[...] = x
    for settle in settles:
        settle()


def final_kernel(aug, per_member, x_ref, state_ref, out_ref):
    rest = jnp.zeros((LANES - x_ref.shape[0], LANES), jnp.float32)
    turned = jnp.transpose(jnp.concatenate([x_ref[...], rest], axis=0))
    parts = split2(turned[0:aug, 0:aug])
    for j in range(0, per_member, 2):
        cut = [state_ref[pl.ds(j + k, aug, stride=per_member), :] for k in range(2)]
        new = mm3(parts, jnp.concatenate(cut, axis=1))
        for k in range(2):
            out_ref[pl.ds(j + k, aug, stride=per_member), :] = new[:, k * LANES:(k + 1) * LANES]


def vspec():
    return pl.BlockSpec(memory_space=pltpu.VMEM)


def sspec():
    return pl.BlockSpec(memory_space=pltpu.SMEM)


def local(ensemble, obs_values, obs_errors, obs_device, obs_cell, obs_order, coupling):
    aug, levels, rows_dev, cols_dev = ensemble.shape
    members = aug - 1
    n_lat, n_lon = lax.axis_size("lat"), lax.axis_size("lon")
    ndev = n_lat * n_lon
    nbatch, nobs = obs_values.shape
    nblocks = coupling.shape[1]
    per_block = nobs // nblocks
    cap = max(1, 2 * nobs // ndev)
    capp = -(-cap // 8) * 8
    digits = digits_of(n_lat, n_lon)
    per_member = levels * rows_dev * cols_dev // LANES
    state = ensemble.reshape(aug * per_member, LANES)
    params = pltpu.CompilerParams(vmem_limit_bytes=VMEM_LIMIT)

    coupled = coupling.reshape(nbatch, 1, nblocks)
    base = nbatch * capp
    rows = base + -(-aug // 16) * 16
    width = aug + 3
    buf, x, source, count, most = pl.pallas_call(
        functools.partial(first_kernel, digits, capp, aug, per_member, base, per_block),
        out_shape=(
            jax.ShapeDtypeStruct((buffer_rows(ndev, capp), LANES), jnp.float32),
            jax.ShapeDtypeStruct((rows, LANES), jnp.float32),
            jax.ShapeDtypeStruct((nbatch, nobs), jnp.int32),
            jax.ShapeDtypeStruct((nbatch,), jnp.int32),
            jax.ShapeDtypeStruct((1,), jnp.int32),
        ),
        in_specs=[vspec()] * 7,
        out_specs=(vspec(), vspec(), vspec(), sspec(), sspec()),
        scratch_shapes=exchange_scratch(digits),
        compiler_params=pltpu.CompilerParams(
            collective_id=0, has_side_effects=True, vmem_limit_bytes=VMEM_LIMIT
        ),
        name="first",
    )(obs_values, obs_errors, obs_device, obs_cell, obs_order, coupled, state)
    z_scratch = pltpu.VMEM((per_block * GROUP, LANES), jnp.float32)

    def stepwise(x, buf, source, count):
        for batch in range(nbatch):
            if batch > 0:
                buf = exchange(x, digits, capp, width, batch, ndev)
            x = pl.pallas_call(
                functools.partial(update_kernel, batch, per_block, members, capp),
                out_shape=jax.ShapeDtypeStruct((rows - (batch + 1) * capp, LANES), jnp.float32),
                in_specs=[sspec(), sspec(), vspec(), vspec()],
                out_specs=vspec(),
                scratch_shapes=[z_scratch],
                compiler_params=params,
                name="update",
            )(source, count, x, buf)
        return x

    def together(x, buf, source, count):
        step_scratch = [pltpu.VMEM((buffer_rows(ndev, capp), LANES), jnp.float32)] + exchange_scratch(digits)
        return pl.pallas_call(
            functools.partial(rest_kernel, digits, capp, width, per_block, members),
            out_shape=jax.ShapeDtypeStruct((rows - base, LANES), jnp.float32),
            in_specs=[sspec(), sspec(), vspec(), vspec()],
            out_specs=vspec(),
            scratch_shapes=[z_scratch] + step_scratch * (nbatch - 1),
            compiler_params=pltpu.CompilerParams(
                collective_id=nbatch, has_side_effects=True, vmem_limit_bytes=VMEM_LIMIT
            ),
            name="rest",
        )(source, count, x, buf)

    if is_grid(digits):
        x = lax.cond(most.reshape(()) <= GROUP, together, stepwise, x, buf, source, count)
    else:
        x = stepwise(x, buf, source, count)

    out = pl.pallas_call(
        functools.partial(final_kernel, aug, per_member),
        out_shape=jax.ShapeDtypeStruct((aug * per_member, LANES), jnp.float32),
        in_specs=[vspec(), vspec()],
        out_specs=vspec(),
        compiler_params=params,
        name="final",
    )(x, state)
    return out.reshape(aug, levels, rows_dev, cols_dev)


def solution(mesh):
    placed = (P(None, None, "lat", "lon"), P(), P(), P(), P(), P(), P(None, None, "lat", "lon"))
    return jax.shard_map(
        local, mesh=mesh, in_specs=placed, out_specs=P(None, None, "lat", "lon"), check_vma=False
    )
```

```python
import functools
import jax
import jax.numpy as jnp
from jax import lax
from jax.experimental import pallas as pl
from jax.experimental.pallas import tpu as pltpu
from jax.sharding import PartitionSpec as P

MESH = pl.DeviceIdType.MESH
GROUP = 32
LANES = 128
PLANE = ((0, 0), (1, 0), (0, 1), (1, 1))
VMEM_LIMIT = 32 * 1024 * 1024


def digits_of(n_lat, n_lon):
    def factors(size):
        out, stride = [], 1
        while size > 1:
            f = 4 if size % 4 == 0 else (2 if size % 2 == 0 else size)
            out.append((stride, f))
            stride, size = stride * f, size // f
        return out
    if (n_lat, n_lon) == (16, 2):
        return [("lat", 4, 4), ("lat", 1, 2), ("lat", 2, 2), ("lon", 1, 2)]
    return [("lon", s, f) for s, f in factors(n_lon)] + [("lat", s, f) for s, f in factors(n_lat)]


def split2(a):
    hi = a.astype(jnp.bfloat16)
    return hi, (a - hi.astype(jnp.float32)).astype(jnp.bfloat16)


def mm3(a, b, dims=((1,), (0,))):
    ah, al = a if isinstance(a, tuple) else split2(a)
    bh, bl = b if isinstance(b, tuple) else split2(b)
    dot = functools.partial(
        lax.dot_general, dimension_numbers=(dims, ((), ())), preferred_element_type=jnp.float32
    )
    return dot(ah, bh) + (dot(ah, bl) + dot(al, bh))


NT = ((1,), (1,))


def pow2_part(value, stride, size):
    return (value >> (stride.bit_length() - 1)) & (size - 1)


def fold_of(cap, width):
    return 24 if cap == 32 and LANES - width >= (width + 1) // 2 else cap


def is_grid(digits):
    return [size for _, _, size in digits] == [4, 2, 2, 2]


class Exchange:
    def __init__(self, digits, cap, width):
        self.digits, self.cap, self.width = digits, cap, width
        self.sent = fold_of(cap, width)
        self.place = {axis: lax.axis_index(axis) for axis in ("lat", "lon")}
        self.mine = [lax.rem(self.place[axis] // stride, size) for axis, stride, size in digits]
        self.weights = [1]
        for _, _, size in digits:
            self.weights.append(self.weights[-1] * size)
        if is_grid(digits):
            self.spread = [(dz, turn) for dz in (2, 1, 3, 0) for turn in PLANE[::-1] if dz or any(turn)]
            self.partners = [((0, dz), (1, dx), (2, dy)) for dz, (dx, dy) in self.spread] + [((3, 1),)]
        else:
            self.partners = [
                ((which, step),) for which, (_, _, size) in enumerate(digits) for step in range(1, size)
            ]

    def peer(self, *moves):
        moved = dict(self.place)
        for which, step in moves:
            axis, stride, size = self.digits[which]
            other = lax.rem(self.mine[which] + step, size)
            moved[axis] = moved[axis] + (other - self.mine[which]) * stride
        return (moved["lat"], moved["lon"])

    def greet(self):
        barrier = pltpu.get_barrier_semaphore()
        for moves in self.partners:
            pl.semaphore_signal(barrier, inc=1, device_id=self.peer(*moves), device_id_type=MESH)

    def await_greetings(self):
        pl.semaphore_wait(pltpu.get_barrier_semaphore(), len(self.partners))

    def place_own(self, chunk, buf_ref):
        width, sent = self.width, self.sent
        half = (width + 1) // 2
        own = sum(digit * weight for digit, weight in zip(self.mine, self.weights))
        if sent < self.cap:
            tail = chunk[24:32]
            lane = lax.broadcasted_iota(jnp.int32, tail.shape, 1)
            low = jnp.where(lane < half, tail, 0.0)
            high = jnp.where((lane >= half) & (lane < width), tail, 0.0)
            buf_ref[own, 0:8] = chunk[0:8] + pltpu.roll(low, width, 1)
            buf_ref[own, 8:16] = chunk[8:16] + pltpu.roll(high, width - half, 1)
            buf_ref[own, 16:24] = chunk[16:24]
        else:
            buf_ref[own] = chunk

    def run(self, buf_ref, send_sem, recv_sem, meanwhile=lambda: None):
        digits, mine, weights, sent = self.digits, self.mine, self.weights, self.sent
        sends = []

        def send(start, count, device):
            slot = len(sends)
            part = buf_ref.at[pl.ds(start, count), pl.ds(0, sent)]
            copy = pltpu.make_async_remote_copy(
                src_ref=part, dst_ref=part, send_sem=send_sem.at[slot], recv_sem=recv_sem.at[slot],
                device_id=device, device_id_type=MESH,
            )
            copy.start()
            sends.append(copy)
            return copy

        if is_grid(digits):
            z, x, y, k = mine
            arriving = {turn: [] for turn in PLANE}
            for dz, (dx, dy) in self.spread:
                own = z + 4 * x + 8 * y + 16 * k
                arriving[dx, dy].append(send(own, 1, self.peer((0, dz), (1, dx), (2, dy))))
            meanwhile()
            last = []
            for dx, dy in PLANE:
                for copy in arriving[dx, dy]:
                    copy.wait_recv()
                start = 4 * lax.rem(x + dx, 2) + 8 * lax.rem(y + dy, 2) + 16 * k
                last.append(send(start, 4, self.peer((3, 1))))
            for copy in last:
                copy.wait_recv()
        else:
            for which, (_, _, size) in enumerate(digits):
                start = sum(mine[i] * weights[i] for i in range(which, len(digits)))
                stage = [send(start, weights[which], self.peer((which, step))) for step in range(1, size)]
                if which == 0:
                    meanwhile()
                for copy in stage:
                    copy.wait_recv()
        if sent < self.cap:
            width = self.width
            half = (width + 1) // 2
            for spot in range(weights[-1]):
                low = pltpu.roll(buf_ref[spot, 0:8], LANES - width, 1)
                high = pltpu.roll(buf_ref[spot, 8:16], LANES - width + half, 1)
                lane = lax.broadcasted_iota(jnp.int32, low.shape, 1)
                buf_ref[spot, 24:32] = jnp.where(lane < half, low, high)

        def settle():
            for copy in sends:
                copy.wait_send()

        return settle


def exchange_kernel(digits, cap, width, x_ref, buf_ref, send_sem, recv_sem):
    trade = Exchange(digits, cap, width)
    trade.greet()
    trade.place_own(x_ref[0:cap, :], buf_ref)
    trade.await_greetings()
    trade.run(buf_ref, send_sem, recv_sem)()


def exchange_scratch(digits):
    copies = 19 if is_grid(digits) else sum(s - 1 for _, _, s in digits)
    return [pltpu.SemaphoreType.DMA((copies,)), pltpu.SemaphoreType.DMA((copies,))]


def exchange(x, digits, cap, width, ident, ndev):
    return pl.pallas_call(
        functools.partial(exchange_kernel, digits, cap, width),
        out_shape=jax.ShapeDtypeStruct((ndev, cap, LANES), jnp.float32),
        in_specs=[vspec()],
        out_specs=vspec(),
        scratch_shapes=exchange_scratch(digits),
        compiler_params=pltpu.CompilerParams(
            collective_id=ident, has_side_effects=True, vmem_limit_bytes=VMEM_LIMIT
        ),
        name="exchange",
    )(x)


def first_kernel(digits, capp, aug, per_member, base, per_block, values_ref, errors_ref,
                 device_ref, cell_ref, order_ref, coupled_ref, state_ref, buf_ref, x_ref, source_ref, count_ref,
                 most_ref, send_sem, recv_sem):
    trade = Exchange(digits, capp, aug + 3)
    trade.greet()
    nbatch, nobs = device_ref.shape
    n_lat, n_lon = lax.axis_size("lat"), lax.axis_size("lon")
    ndev = n_lat * n_lon
    me = lax.axis_index("lat") * n_lon + lax.axis_index("lon")
    earlier = (
        lax.broadcasted_iota(jnp.int32, (nobs, nobs), 0) < lax.broadcasted_iota(jnp.int32, (nobs, nobs), 1)
    ).astype(jnp.float32).astype(jnp.bfloat16)

    def ranks(flags):
        return jnp.dot(flags.astype(jnp.bfloat16), earlier, preferred_element_type=jnp.float32)

    def coupled_of(batch):
        return (coupled_ref[batch] > 0).astype(jnp.float32)

    def fill():
        owned = (device_ref[...] == me).astype(jnp.float32)
        rank = ranks(owned)
        slot = lax.broadcasted_iota(jnp.int32, (capp, nobs), 0).astype(jnp.float32)
        lane = lax.broadcasted_iota(jnp.int32, (capp, LANES), 1)
        cells = []
        most = jnp.zeros((1, 1), jnp.float32)
        for batch in range(nbatch):
            most = jnp.maximum(most, jnp.sum(coupled_of(batch), axis=1, keepdims=True))
        for batch in range(nbatch):
            row = slice(batch, batch + 1)
            chosen = (rank[row] == slot) & (owned[row] > 0)

            def total(ref):
                return jnp.sum(jnp.where(chosen, ref[row, :].astype(jnp.float32), 0.0), axis=1, keepdims=True)

            cells.append(total(cell_ref))
            x_ref[batch * capp:(batch + 1) * capp, :] = jnp.where(
                lane == aug, total(values_ref), jnp.where(
                    lane == aug + 1, total(errors_ref), jnp.where(lane == aug + 2, most, 0.0)
                )
            )
        cell = jnp.concatenate(cells, axis=0).astype(jnp.int32)
        wide = 2 * LANES
        spot = lax.broadcasted_iota(jnp.int32, (nbatch * capp, wide), 1)
        picked = jnp.zeros((nbatch * capp, aug), jnp.float32)
        for j in range(0, per_member, 2):
            cut = jnp.concatenate(
                [state_ref[pl.ds(j + k, aug, stride=per_member), :] for k in range(2)], axis=1
            )
            mark = (spot + j * LANES == cell).astype(jnp.float32).astype(jnp.bfloat16)
            for _ in range(3):
                part = cut.astype(jnp.bfloat16)
                picked = picked + lax.dot_general(
                    mark, part, (NT, ((), ())), preferred_element_type=jnp.float32
                )
                cut = cut - part.astype(jnp.float32)
        x_ref[0:base, 0:aug] = picked
        return x_ref[0:capp, :]

    def meanwhile():
        square = (x_ref.shape[0] - base, LANES)
        x_ref[base:, :] = (
            lax.broadcasted_iota(jnp.int32, square, 0) == lax.broadcasted_iota(jnp.int32, square, 1)
        ).astype(jnp.float32)
        names = lax.broadcasted_iota(jnp.int32, (ndev, nobs), 0)
        names_obs = lax.broadcasted_iota(jnp.int32, (nobs, nobs), 0)
        nblocks = coupled_ref.shape[2]
        block = lax.broadcasted_iota(jnp.int32, (nblocks, nobs), 0) * per_block
        member = lax.broadcasted_iota(jnp.int32, (nblocks, nobs), 1)
        widen = ((member >= block) & (member < block + per_block)).astype(jnp.float32).astype(jnp.bfloat16)
        for batch in range(nbatch):
            device = device_ref[batch:batch + 1, :]
            held = (device == names).astype(jnp.float32)
            rank = jnp.sum(held * ranks(held), axis=0, keepdims=True)
            place = {"lat": device >> (n_lon.bit_length() - 1), "lon": device & (n_lon - 1)}
            slab, weight = jnp.zeros_like(device), 1
            for axis, stride, size in digits:
                slab = slab + pow2_part(place[axis], stride, size) * weight
                weight *= size
            pos = slab * capp + rank.astype(jnp.int32)
            part = lax.broadcasted_iota(jnp.int32, (8, nobs), 0)
            parts = jnp.where(part == 0, pos & 63, jnp.where(part == 1, (pos >> 6) & 63, pos >> 12))
            parts = jnp.where(part < 3, parts, 0).astype(jnp.float32).astype(jnp.bfloat16)
            named = (order_ref[batch:batch + 1, :] == names_obs).astype(jnp.float32).astype(jnp.bfloat16)
            ordered = jnp.dot(parts, named, preferred_element_type=jnp.float32)
            coupled = jnp.dot(coupled_of(batch).astype(jnp.bfloat16), widen, preferred_element_type=jnp.float32)
            goes = (ranks(coupled) == names_obs.astype(jnp.float32)) & (coupled > 0.5)
            packed = lax.dot_general(
                ordered.astype(jnp.bfloat16), goes.astype(jnp.float32).astype(jnp.bfloat16), (NT, ((), ())),
                preferred_element_type=jnp.float32,
            ).astype(jnp.int32)
            source_ref[batch:batch + 1, :] = packed[0:1] + 64 * packed[1:2] + 4096 * packed[2:3]
            count_ref[batch] = jnp.sum(coupled_of(batch)).astype(jnp.int32)

    trade.place_own(fill(), buf_ref)
    trade.await_greetings()
    settle = trade.run(buf_ref, send_sem, recv_sem, meanwhile)
    most = buf_ref[0, 0:8]
    for spot in range(1, ndev):
        most = jnp.maximum(most, buf_ref[spot, 0:8])
    lane = lax.broadcasted_iota(jnp.int32, (8, LANES), 1)
    most_ref[0] = jnp.max(jnp.where(lane == aug + 2, most, 0.0)).astype(jnp.int32)
    settle()


def group_update(z, valid, x, per_block, members):
    lane = lax.broadcasted_iota(jnp.int32, (GROUP, LANES), 1)
    is_member = (lane >= 1) & (lane <= members)
    z = list(z)
    hs, vs, ws = [], [], []
    for i in range(per_block):
        p = z[i]
        h = jnp.where(is_member, p, 0.0)
        s = jnp.sum(h * h, axis=1, keepdims=True) * (1.0 / (members - 1))
        y = p[:, members + 1:members + 2]
        r = p[:, members + 2:members + 3]
        q = s + r
        c = 1.0 / ((members - 1) * q)
        a = 1.0 / (1.0 + jnp.sqrt(r / q))
        d = y - p[:, 0:1]
        v = jnp.where(lane == 0, c * d, -(a * c) * h)
        for j in range(i + 1, per_block):
            z[j] = z[j] + v * jnp.sum(h * z[j], axis=1, keepdims=True)
        w = h
        for j in range(i):
            w = w + ws[j] * jnp.sum(h * vs[j], axis=1, keepdims=True)
        vs.append(v)
        ws.append(w)
    half = GROUP // 2
    size = per_block * half
    row_id = lax.broadcasted_iota(jnp.int32, (size, size), 0)
    col_id = lax.broadcasted_iota(jnp.int32, (size, size), 1)
    differ = (row_id ^ col_id) & (half - 1)
    ahead = (row_id & (half - 1)) < (col_id & (half - 1))
    levels = half.bit_length() - 1
    vs = [v * valid for v in vs]
    cuts = [slice(0, half), slice(half, GROUP)]
    v_half = [split2(jnp.concatenate([v[cut] for v in vs], axis=0)) for cut in cuts]
    w_half = [split2(jnp.concatenate([w[cut] for w in ws], axis=0)) for cut in cuts]
    upper = [mm3(v, w, NT) for v, w in zip(v_half, w_half)]
    inverse = [
        jnp.where(row_id == col_id, 1.0, jnp.where(ahead & (differ == 1), u, 0.0)) for u in upper
    ]
    x_parts = split2(x)
    asides = [
        lambda: mm3(x_parts, w_half[0], NT), lambda: mm3(x_parts, w_half[1], NT),
        lambda: split2(mm3(v_half[0], w_half[1], NT)),
    ]
    done = []
    for level in range(1, levels):
        pairs = ahead & (differ >= (1 << level)) & (differ < (2 << level))
        parts = [split2(i) for i in inverse]
        inner = [mm3(p, jnp.where(pairs, u, 0.0)) for p, u in zip(parts, upper)]
        if len(done) < len(asides):
            done.append(asides[len(done)]())
        inverse = [i + mm3(m, p) for i, m, p in zip(inverse, inner, parts)]
    done.extend(aside() for aside in asides[len(done):])
    seen_first, seen_second, across = done
    first = split2(mm3(seen_first, inverse[0]))
    second = mm3(seen_second + mm3(first, across), inverse[1])
    return x + (mm3(first, v_half[0]) + mm3(second, v_half[1]))


def group_of(source_ref, buf_ref, z_ref, batch, total, start, x, per_block, members):
    cap = buf_ref.shape[1]
    shift = cap.bit_length() - 1

    @pl.loop(0, GROUP, unroll=8)
    def _(b):
        for i in range(per_block):
            row = source_ref[batch, (start + b) * per_block + i]
            z_ref[pl.ds(i * GROUP + b, 1), :] = buf_ref[row >> shift, pl.ds(row & (cap - 1), 1), :]

    valid = (start + lax.broadcasted_iota(jnp.int32, (GROUP, 1), 0) < total).astype(jnp.float32)
    z = [z_ref[i * GROUP:(i + 1) * GROUP, :] for i in range(per_block)]
    return group_update(z, valid, x, per_block, members)


def update_kernel(batch, per_block, members, capp, source_ref, count_ref, x_ref, buf_ref, out_ref, z_ref):
    out_ref[...] = x_ref[capp:, :]
    total = count_ref[batch]

    @pl.loop(0, (total + GROUP - 1) // GROUP)
    def _(group):
        out_ref[...] = group_of(
            source_ref, buf_ref, z_ref, batch, total, group * GROUP, out_ref[...], per_block, members
        )


def rest_kernel(digits, cap, width, per_block, members, source_ref, count_ref, x_ref, buf_ref, out_ref, z_ref, *more):
    nbatch = len(more) // 3 + 1
    trade = Exchange(digits, cap, width)
    trade.greet()
    x = x_ref[...]
    settles = []
    for batch in range(nbatch):
        x = group_of(source_ref, buf_ref, z_ref, batch, count_ref[batch], 0, x[cap:], per_block, members)
        if batch == 0:
            trade.await_greetings()
        if batch + 1 < nbatch:
            buf_ref, send_sem, recv_sem = more[3 * batch:3 * batch + 3]
            trade.place_own(x[0:cap], buf_ref)
            settles.append(trade.run(buf_ref, send_sem, recv_sem))
    out_ref[...] = x
    for settle in settles:
        settle()


def final_kernel(aug, per_member, x_ref, state_ref, out_ref):
    rest = jnp.zeros((LANES - x_ref.shape[0], LANES), jnp.float32)
    turned = jnp.transpose(jnp.concatenate([x_ref[...], rest], axis=0))
    parts = split2(turned[0:aug, 0:aug])
    for j in range(0, per_member, 2):
        cut = [state_ref[pl.ds(j + k, aug, stride=per_member), :] for k in range(2)]
        new = mm3(parts, jnp.concatenate(cut, axis=1))
        for k in range(2):
            out_ref[pl.ds(j + k, aug, stride=per_member), :] = new[:, k * LANES:(k + 1) * LANES]


def vspec():
    return pl.BlockSpec(memory_space=pltpu.VMEM)


def sspec():
    return pl.BlockSpec(memory_space=pltpu.SMEM)


def local(ensemble, obs_values, obs_errors, obs_device, obs_cell, obs_order, coupling):
    aug, levels, rows_dev, cols_dev = ensemble.shape
    members = aug - 1
    n_lat, n_lon = lax.axis_size("lat"), lax.axis_size("lon")
    ndev = n_lat * n_lon
    nbatch, nobs = obs_values.shape
    nblocks = coupling.shape[1]
    per_block = nobs // nblocks
    cap = max(1, 2 * nobs // ndev)
    capp = -(-cap // 8) * 8
    digits = digits_of(n_lat, n_lon)
    per_member = levels * rows_dev * cols_dev // LANES
    state = ensemble.reshape(aug * per_member, LANES)
    params = pltpu.CompilerParams(vmem_limit_bytes=VMEM_LIMIT)

    coupled = coupling.reshape(nbatch, 1, nblocks)
    base = nbatch * capp
    rows = base + -(-aug // 16) * 16
    width = aug + 3
    buf, x, source, count, most = pl.pallas_call(
        functools.partial(first_kernel, digits, capp, aug, per_member, base, per_block),
        out_shape=(
            jax.ShapeDtypeStruct((ndev, capp, LANES), jnp.float32),
            jax.ShapeDtypeStruct((rows, LANES), jnp.float32),
            jax.ShapeDtypeStruct((nbatch, nobs), jnp.int32),
            jax.ShapeDtypeStruct((nbatch,), jnp.int32),
            jax.ShapeDtypeStruct((1,), jnp.int32),
        ),
        in_specs=[vspec()] * 7,
        out_specs=(vspec(), vspec(), vspec(), sspec(), sspec()),
        scratch_shapes=exchange_scratch(digits),
        compiler_params=pltpu.CompilerParams(
            collective_id=0, has_side_effects=True, vmem_limit_bytes=VMEM_LIMIT
        ),
        name="first",
    )(obs_values, obs_errors, obs_device, obs_cell, obs_order, coupled, state)
    z_scratch = pltpu.VMEM((per_block * GROUP, LANES), jnp.float32)

    def stepwise(x, buf, source, count):
        for batch in range(nbatch):
            if batch > 0:
                buf = exchange(x, digits, capp, width, batch, ndev)
            x = pl.pallas_call(
                functools.partial(update_kernel, batch, per_block, members, capp),
                out_shape=jax.ShapeDtypeStruct((rows - (batch + 1) * capp, LANES), jnp.float32),
                in_specs=[sspec(), sspec(), vspec(), vspec()],
                out_specs=vspec(),
                scratch_shapes=[z_scratch],
                compiler_params=params,
                name="update",
            )(source, count, x, buf)
        return x

    def together(x, buf, source, count):
        step_scratch = [pltpu.VMEM((ndev, capp, LANES), jnp.float32)] + exchange_scratch(digits)
        return pl.pallas_call(
            functools.partial(rest_kernel, digits, capp, width, per_block, members),
            out_shape=jax.ShapeDtypeStruct((rows - base, LANES), jnp.float32),
            in_specs=[sspec(), sspec(), vspec(), vspec()],
            out_specs=vspec(),
            scratch_shapes=[z_scratch] + step_scratch * (nbatch - 1),
            compiler_params=pltpu.CompilerParams(
                collective_id=nbatch, has_side_effects=True, vmem_limit_bytes=VMEM_LIMIT
            ),
            name="rest",
        )(source, count, x, buf)

    if is_grid(digits):
        x = lax.cond(most.reshape(()) <= GROUP, together, stepwise, x, buf, source, count)
    else:
        x = stepwise(x, buf, source, count)

    out = pl.pallas_call(
        functools.partial(final_kernel, aug, per_member),
        out_shape=jax.ShapeDtypeStruct((aug * per_member, LANES), jnp.float32),
        in_specs=[vspec(), vspec()],
        out_specs=vspec(),
        compiler_params=params,
        name="final",
    )(x, state)
    return out.reshape(aug, levels, rows_dev, cols_dev)


def solution(mesh):
    placed = (P(None, None, "lat", "lon"), P(), P(), P(), P(), P(), P(None, None, "lat", "lon"))
    return jax.shard_map(
        local, mesh=mesh, in_specs=placed, out_specs=P(None, None, "lat", "lon"), check_vma=False
    )
```
